256 devices in a mesh: hemi: 2 (over core), dev: 128 (over z, y, x).
Axes of the slice: x: 4, y: 4, z: 8, core: 2. Of those that a mesh axis runs over, the one named last changes fastest.
Arguments:
- spectrum: float32 [384, 512, 256], P(None, 'dev', 'hemi'), may hold values from 0.05 to 1
- wind_speed: float32 [512, 256], P('dev', 'hemi'), may hold values from 0.2 to 1
- src_counts: int32 [512, 256], P('dev', 'hemi'), may hold values from 1 to 3
- ocean_mask: int32 [512, 256], replicated, may hold values 0 or 1
- growth: float32 [384], replicated, may hold values from 0.1 to 0.6
- quadruplet: int32 [2, 384, 384], replicated, may hold values from 0 to 1, as said below
- courant: float32 [16], replicated, may hold values from 0.4 to 0.95
- freq_counts: int32 [16], replicated, may hold values from 1 to 4
Outputs:
- spectrum_next: float32 [384, 512, 256], P(None, 'dev', 'hemi')
The draws below stay inside these ranges and needn't reach their ends.
Inputs may be any that keep to these rules, and one draw needn't show every extreme that they name: Each row of quadruplet[0] and of quadruplet[1] holds a single 1.
All inputs are finite; a program needn't handle non-finite values.
Results may differ from the reference program's by a relative error of at most 0.0003.
Values sent between devices are 32-bit elements; how exact they have to be, the bound alone decides.
No kernel may reach another device: no remote copies, remote signals or barrier semaphores. Data moves between devices by JAX's collectives and lax.ppermute only.
A program may use at most 64 MiB of HBM per device.

```python
import math
import jax
import jax.numpy as jnp
from jax import lax

ND = 24
NF = 16
K = 384
LON_DEV = 4
SRC_MAX = 3
SUB_MAX = 4
NLON = 512
NLAT = 256
N_DEV = 128


def draw_quadruplet(key, part):
    key = jax.random.fold_in(key, 11)
    key_freq, key_dir = jax.random.split(key)
    step_freq = jax.random.randint(key_freq, (2, NF), 1, 3)
    step_dir = jax.random.randint(key_dir, (2, NF), 1, ND // 2 + 1)
    component = jnp.arange(ND * NF)
    frequency = component // ND
    direction = component % ND
    sign_side = jnp.array([1, -1], dtype=jnp.int32)[:, None]
    target_freq = jnp.clip(frequency[None, :] + sign_side * step_freq[:, frequency], 0, NF - 1)
    target_dir = (direction[None, :] + sign_side * step_dir[:, frequency]) % ND
    target = target_freq * ND + target_dir
    return (target[:, :, None] == component[None, None, :]).astype(jnp.int32)


def draw_freq_counts(key, part):
    key = jax.random.fold_in(key, 12)
    key_level, key_pick = jax.random.split(key)
    counts = jax.random.randint(key_level, (NF,), 1, SUB_MAX + 1)
    chosen = jax.random.randint(key_pick, (), 0, NF)
    return counts.at[chosen].set(SUB_MAX).astype(jnp.int32)


def draw_src_counts(key, part):
    key = jax.random.fold_in(key, 13)
    key_level, key_point, key_pick = jax.random.split(key, 3)
    blocks = NLON // LON_DEV
    level_of = jax.random.randint(key_level, (blocks,), 1, SRC_MAX + 1)
    chosen = jax.random.randint(key_pick, (), 0, blocks)
    level_of = level_of.at[chosen].set(SRC_MAX)
    level_rows = jnp.repeat(level_of, LON_DEV)[:, None]
    raw_draw = jax.random.randint(key_point, (NLON, NLAT), 0, 840)
    counts = 1 + raw_draw % level_rows
    return counts.at[chosen * LON_DEV, 0].set(SRC_MAX).astype(jnp.int32)


def set_ends(values, own_key, low, high):
    dims = values.shape
    spot = [jax.random.randint(jax.random.fold_in(own_key, axis), (), 0, dims[axis]) for axis in range(len(dims))]
    values = values.at[tuple(spot)].set(low)
    longest = dims.index(max(dims))
    spot[longest] = (spot[longest] + 1) % dims[longest]
    return values.at[tuple(spot)].set(high)


def block_levels(key, dims, shards, smallest, top_value):
    loudness = 1.0
    for axis_at, shards_of in shards:
        heights = jax.random.uniform(jax.random.fold_in(jax.random.fold_in(key, 6), axis_at), (shards_of,), jnp.float32, smallest / len(shards), top_value / len(shards))
        loudness = loudness * jnp.repeat(jnp.exp(heights), dims[axis_at] // shards_of).reshape((-1,) + (1,) * (len(dims) - 1 - axis_at))
    return loudness


def setup_inputs(seed: int = 0) -> dict:
    key_of = jax.random.split(jax.random.key(seed), 9)
    spectrum = jnp.clip(jnp.exp(math.log(1.0) - 2.9957323 * jax.random.uniform(key_of[0], (K, NLON, NLAT), jnp.float32) ** block_levels(key_of[0], (K, NLON, NLAT), ((1, 128), (2, 2)), -0.2, 0.2)), 0.05, 1.0)
    wind_speed = jnp.clip(0.2 + 0.8 * jax.random.uniform(key_of[1], (NLON, NLAT), jnp.float32) ** block_levels(key_of[1], (NLON, NLAT), ((0, 128), (1, 2)), -0.2, 0.2), 0.2, 1.0)
    src_counts = draw_src_counts(jax.random.fold_in(key_of[8], 71), 0)
    ocean_mask = set_ends((jax.random.randint(key_of[3], (NLON, NLAT), 0, 8) < 7).astype(jnp.int32), jax.random.fold_in(key_of[3], 1), 0, 1)
    growth = jnp.clip(jnp.exp(jax.random.uniform(key_of[4], (K,), jnp.float32, math.log(0.1), math.log(0.6))), 0.1, 0.6)
    quadruplet = draw_quadruplet(jax.random.fold_in(key_of[8], 71), 0)
    courant = jnp.clip(jax.random.uniform(key_of[6], (NF,), jnp.float32, 0.4, 0.95), 0.4, 0.95)
    freq_counts = draw_freq_counts(jax.random.fold_in(key_of[8], 71), 0)
    return dict(spectrum=spectrum, wind_speed=wind_speed, src_counts=src_counts, ocean_mask=ocean_mask, growth=growth, quadruplet=quadruplet, courant=courant, freq_counts=freq_counts)


coupling = 0.25
breaking = 0.5
spread = 0.7


def speeds(courant, comp_total):
    component = jnp.arange(comp_total)
    direction = (component % ND).astype(jnp.float32)
    angles = 2.0 * jnp.pi * (direction + 0.5) / ND
    magnitude = spread * courant[component // ND]
    return magnitude * jnp.cos(angles), magnitude * jnp.sin(angles)


def upwind(level, west_side, east_side, south_side, north_side, cx_rate, cy_rate, ocean):
    return ocean * (level - jnp.maximum(cx_rate, 0.0) * (level - west_side) - jnp.maximum(-cx_rate, 0.0) * (level - east_side) - jnp.maximum(cy_rate, 0.0) * (level - south_side) - jnp.maximum(-cy_rate, 0.0) * (level - north_side))


def source_terms(energy, wind_speed, src_counts, ocean, growth, quad_pair, quad_sum, trip_count):
    comp_total = energy.shape[0]
    step_size = 1.0 / src_counts.astype(jnp.float32)
    energy = energy * ocean[None, :]

    def substep(cycle_idx, energy):
        paired = jnp.dot(quad_pair, energy, precision=lax.Precision.HIGHEST, preferred_element_type=jnp.float32)
        plus_side = paired[:comp_total]
        minus_side = paired[comp_total:]
        quad_term = energy * energy * (plus_side + minus_side) - 2.0 * energy * plus_side * minus_side
        spread_back = lax.dot_general(quad_sum, quad_term, (((0,), (0,)), ((), ())), precision=lax.Precision.HIGHEST, preferred_element_type=jnp.float32)
        tendency = growth[:, None] * wind_speed[None, :] * energy + coupling * (spread_back - 2.0 * quad_term) - breaking * energy * energy
        updated = ocean[None, :] * (energy + step_size[None, :] * tendency)
        return jnp.where((cycle_idx < src_counts)[None, :], updated, energy)

    return lax.fori_loop(0, trip_count, substep, energy)


def reference(spectrum, wind_speed, src_counts, ocean_mask, growth, quadruplet, courant, freq_counts):
    comp_total = ND * NF
    ocean = ocean_mask.astype(jnp.float32)
    quad_float = quadruplet.astype(jnp.float32)
    quad_pair = quad_float.reshape(2 * comp_total, comp_total)
    quad_sum = quad_float[0] + quad_float[1]
    blocks = N_DEV
    points = LON_DEV * NLAT
    energy_blk = jnp.moveaxis(spectrum.reshape(comp_total, blocks, points), 1, 0)
    wind_blk = wind_speed.reshape(blocks, points)
    count_blk = src_counts.reshape(blocks, points)
    ocean_blk = ocean.reshape(blocks, points)

    def block_source(operands):
        energy, wind_part, count_part, ocean_part = operands
        return source_terms(energy, wind_part, count_part, ocean_part, growth, quad_pair, quad_sum, SRC_MAX)

    sourced = lax.map(block_source, (energy_blk, wind_blk, count_blk, ocean_blk))
    energy = jnp.moveaxis(sourced, 0, 1).reshape(comp_total, NLON, NLAT)
    cx_all, cy_all = speeds(courant, comp_total)
    trip_table = freq_counts[jnp.arange(comp_total) // ND]

    def one_component(operands):
        level, cx_rate, cy_rate, trip_count = operands

        def substep(cycle_idx, level):
            west_side = jnp.roll(level, 1, axis=0)
            east_side = jnp.roll(level, -1, axis=0)
            padded = jnp.pad(level, ((0, 0), (1, 1)))
            return upwind(level, west_side, east_side, padded[:, :-2], padded[:, 2:], cx_rate, cy_rate, ocean)

        return lax.fori_loop(0, trip_count, substep, level)

    return lax.map(one_component, (energy, cx_all, cy_all, trip_table))
```

```python
import functools
import math

import jax
import jax.numpy as jnp
from jax import lax
from jax.experimental import pallas as pl
from jax.experimental.pallas import tpu as pltpu
from jax.sharding import PartitionSpec as P

ND = 24
NF = 16
K = ND * NF
LON = 4
LAT = 128
PTS = LON * LAT
SRC_MAX = 3
SUB_MAX = 4
HALF = K // 2
GROUP = 6 * NF
coupling = 0.25
breaking = 0.5
spread = 0.7
MIB = 1024 * 1024
SIDE = 4


def direction(j, hemi):
    return lax.rem(18 + j + 12 * hemi, ND)


def split(value):
    high = value.astype(jnp.bfloat16)
    low = (value - high.astype(jnp.float32)).astype(jnp.bfloat16)
    return high, low


def role(hemi, dev):
    x = lax.rem(dev, SIDE)
    return (x == 0) & (hemi == 0) | (x == SIDE - 1) & (hemi == 1)


def reorder(slot, hemi, energy, out):
    forward = hemi if slot == 0 else 1 - hemi
    for jj in range(12):
        d = direction(jj + 12 * slot, hemi)
        for n in range(LON):
            lon = n + forward * (LON - 1 - 2 * n)
            at = n * HALF + jj * NF
            out[at:at + NF, :] = energy[pl.ds(lon * K + d, NF, stride=ND), :]


def source_terms(
    hemi, dev, ocean_ref, growth_ref, wind_ref, count_ref, quad_ref, spec_ref, waits,
    gather_m, scatter_m, energy, parts, paired, terms, moved, grow,
):
    nt = (((1,), (1,)), ((), ()))
    eye = (
        lax.broadcasted_iota(jnp.int32, (K, K), 0) == lax.broadcasted_iota(jnp.int32, (K, K), 1)
    ).astype(jnp.float32)
    eye_bf = eye.astype(jnp.bfloat16)
    waits["small"]()
    rest = jnp.broadcast_to(growth_ref[...].reshape(1, K), (LAT, K))
    column = None
    for _ in range(3):
        part = rest.astype(jnp.bfloat16)
        rest = rest - part.astype(jnp.float32)
        term = lax.dot_general(eye_bf, part, nt, preferred_element_type=jnp.float32)
        column = term if column is None else column + term
    grow[...] = column

    winds = []
    oceans = []
    counts = []
    for lon in range(LON):
        winds.append(wind_ref[lon:lon + 1, :])
        counts.append(count_ref[lon:lon + 1, :])
        row = ocean_ref[pl.ds(LON * lax.rem(dev, 2) + lon, 1), :].astype(jnp.float32)
        oceans.append(jnp.where(hemi == 0, row[:, :LAT], row[:, LAT:]))
    steps = [oceans[lon] / counts[lon].astype(jnp.float32) for lon in range(LON)]

    waits["quad"]()
    sides = []
    for side in range(2):
        rows = quad_ref[side * K:(side + 1) * K, :].astype(jnp.float32).astype(jnp.bfloat16)
        gather_m[side * K:(side + 1) * K, :K] = rows
        gather_m[side * K:(side + 1) * K, K:] = rows
        sides.append(rows)
    back = lax.dot_general(eye_bf, sides[0] + sides[1], nt, preferred_element_type=jnp.float32)
    back = (coupling * (back - 2.0 * eye)).astype(jnp.bfloat16)
    scatter_m[:, :K] = back
    scatter_m[:, K:] = back

    waits["spec"]()
    for i in range(K // NF):
        for lon in range(LON):
            cols = slice(lon * LAT, (lon + 1) * LAT)
            value = spec_ref[pl.ds(i * NF * LON + lon, NF, stride=LON), :] * oceans[lon]
            energy[lon * K + i * NF:lon * K + (i + 1) * NF, :] = value
            high, low = split(value)
            parts[i * NF:(i + 1) * NF, cols] = high
            parts[K + i * NF:K + (i + 1) * NF, cols] = low

    def substep(cycle, carry):
        paired[...] = jnp.dot(gather_m[...], parts[...], preferred_element_type=jnp.float32)

        def quad_rows(i, carry):
            at = pl.multiple_of(i * NF, NF)
            below = pl.multiple_of(K + i * NF, NF)
            for lon in range(LON):
                cols = slice(lon * LAT, (lon + 1) * LAT)
                value = energy[pl.ds(lon * K + at, NF), :]
                plus = paired[pl.ds(at, NF), cols]
                minus = paired[pl.ds(below, NF), cols]
                term = value * (value * (plus + minus) - 2.0 * (plus * minus))
                high, low = split(term)
                terms[pl.ds(at, NF), cols] = high
                terms[pl.ds(below, NF), cols] = low
            return carry

        lax.fori_loop(0, K // NF, quad_rows, 0, unroll=4)
        moved[...] = jnp.dot(scatter_m[...], terms[...], preferred_element_type=jnp.float32)

        def update_rows(i, carry):
            at = pl.multiple_of(i * NF, NF)
            below = pl.multiple_of(K + i * NF, NF)
            rate = grow[pl.ds(at, NF), :]
            for lon in range(LON):
                cols = slice(lon * LAT, (lon + 1) * LAT)
                value = energy[pl.ds(lon * K + at, NF), :]
                tendency = value * (rate * winds[lon] - breaking * value)
                tendency = tendency + moved[pl.ds(at, NF), cols]
                value = jnp.where(cycle < counts[lon], value + steps[lon] * tendency, value)
                energy[pl.ds(lon * K + at, NF), :] = value
                high, low = split(value)
                parts[pl.ds(at, NF), cols] = high
                parts[pl.ds(below, NF), cols] = low
            return carry

        lax.fori_loop(0, K // NF, update_rows, 0, unroll=4)
        return carry

    lax.fori_loop(0, SRC_MAX, substep, 0)


def source_kernel(late, spec, wind, count, growth, quad, ocean, *refs):
    first, second = refs[1:3] if late else refs[:2]
    scratch = refs[3:] if late else refs[2:]
    spec_v, wind_v, count_v, growth_v, quad_v, ocean_v, first_v, second_v, sems = scratch[:9]
    work = scratch[9:]
    hemi = lax.axis_index("hemi")
    dev = lax.axis_index("dev")
    mine = role(hemi, dev) if late else jnp.logical_not(role(hemi, dev))

    @pl.when(mine)
    def _():
        block = pl.multiple_of(dev // 2 * 8, 8)
        small = [
            pltpu.make_async_copy(growth, growth_v, sems.at[2]),
            pltpu.make_async_copy(wind, wind_v, sems.at[3]),
            pltpu.make_async_copy(count, count_v, sems.at[4]),
            pltpu.make_async_copy(ocean.at[pl.ds(block, 8), :], ocean_v, sems.at[5]),
        ]
        large = {
            "quad": pltpu.make_async_copy(quad, quad_v, sems.at[0]),
            "spec": pltpu.make_async_copy(spec, spec_v, sems.at[1]),
        }
        large["quad"].start()
        for copy in small:
            copy.start()
        large["spec"].start()

        def wait_small():
            for copy in small:
                copy.wait()

        waits = {"small": wait_small, "quad": large["quad"].wait, "spec": large["spec"].wait}
        source_terms(
            hemi, dev, ocean_v, growth_v, wind_v, count_v, quad_v, spec_v, waits, *work,
        )
        outs = []
        for slot, (source, target) in enumerate(((first_v, first), (second_v, second))):
            reorder(slot, hemi, work[2], source)
            copy = pltpu.make_async_copy(source, target, sems.at[6 + slot])
            copy.start()
            outs.append(copy)
        for copy in outs:
            copy.wait()


BATCH = (6, 3)


def fine(value, active):
    return value if active is None else jnp.where(active, value, 0.0)


def total(*terms):
    terms = [term for term in terms if term is not None]
    if not terms:
        return None
    out = terms[0]
    for term in terms[1:]:
        out = out + term
    return out


def times(rate, value):
    return None if value is None else rate * value


def advance(slot, hemi, courant_ref, times_ref, masks_ref, load, store, which=(1, 0)):
    forward = hemi if slot == 0 else 1 - hemi
    lanes = slice(hemi * LAT, (hemi + 1) * LAT)
    far_lanes = slice((1 - hemi) * LAT, (2 - hemi) * LAT)
    masks = []
    far_masks = []
    for n in range(-LON, LON):
        at = LON + (n if forward == 0 else LON - 1 - n)
        masks.append(jnp.broadcast_to(masks_ref[at:at + 1, lanes], (8, LAT)))
        far_masks.append(jnp.broadcast_to(masks_ref[at:at + 1, far_lanes], (8, LAT)))
    lane = lax.broadcasted_iota(jnp.int32, (8, LAT), 1)
    row8 = lax.broadcasted_iota(jnp.int32, (8, LAT), 0)
    rates = []
    for half in range(2):
        courant = jnp.zeros((8, LAT), jnp.float32)
        count = jnp.zeros((8, LAT), jnp.int32)
        for r in range(8):
            courant = jnp.where(row8 == r, courant_ref[half * 8 + r], courant)
            count = jnp.where(row8 == r, times_ref[half * 8 + r], count)
        rates.append((spread * courant, [None] + [count > t for t in range(1, SUB_MAX)]))
    for toward in which:
        up = hemi if toward == 0 else 1 - hemi
        shift = 1 if up else LAT - 1
        edge = lane == (0 if up else LAT - 1)
        batch = BATCH[toward]
        for half in range(2):
            speed, active = rates[half]
            for first in range(0, 6, batch):
                groups = []
                for i in range(first, first + batch):
                    jj = i + (6 * toward if slot == 0 else 6 * (1 - toward))
                    angle = 2.0 * math.pi * ((18 + jj + 12 * slot) % ND + 0.5) / ND
                    cx = speed * abs(math.cos(angle))
                    cy = speed * abs(math.sin(angle))
                    base = jj * NF + half * 8
                    cross = i * NF + half * 8
                    groups.append((base, cross, cx, cy, 1.0 - cx - cy, load(base), [None] * (2 * LON)))
                for t in range(SUB_MAX):
                    for n in range(2 * LON - 1, t, -1):
                        for base, cross, cx, cy, stay, level, far in groups:
                            rolled = None if level[n] is None else pltpu.roll(level[n], shift, 1)
                            south = None if rolled is None else jnp.where(edge, 0.0, rolled)
                            value = total(times(stay, level[n]), times(cx, level[n - 1]), times(cy, south))
                            if toward:
                                inflow = None
                                if far[n] is not None:
                                    inflow = jnp.where(edge, rolled, pltpu.roll(far[n], shift, 1))
                                elif rolled is not None:
                                    inflow = jnp.where(edge, rolled, 0.0)
                                other = total(times(stay, far[n]), times(cx, far[n - 1]), times(cy, inflow))
                                if other is not None:
                                    other = far_masks[n] * other
                                    if t:
                                        old = 0.0 if far[n] is None else far[n]
                                        other = jnp.where(active[t], other, old)
                                    far[n] = other
                            if value is not None:
                                value = masks[n] * value
                                if t:
                                    old = 0.0 if level[n] is None else level[n]
                                    value = jnp.where(active[t], value, old)
                                level[n] = value
                for base, cross, cx, cy, stay, level, far in groups:
                    store(base, level[LON:], cross, far[LON:] if toward else None)


def own_rows(base, n):
    return slice(n * HALF + base, n * HALF + base + 8)


def cross_rows(cross, n):
    return slice(n * GROUP + cross, n * GROUP + cross + 8)


def own_kernel(
    courant_ref, times_ref, ocean, first, first_late, second, out0, out1, cross0, cross1, masks,
    first_v, second_v, ocean_v, sems,
):
    hemi = lax.axis_index("hemi")
    dev = lax.axis_index("dev")
    n_dev = lax.axis_size("dev")
    late = role(hemi, dev)
    start = lax.rem(dev + n_dev - 1, n_dev)
    block = start // 2
    blocks = n_dev * LON // 8
    copies = []
    for i in range(2):
        at = pl.multiple_of(lax.rem(block + i, blocks) * 8, 8)
        copies.append(
            pltpu.make_async_copy(
                ocean.at[pl.ds(at, 8), :], ocean_v.at[pl.ds(8 * i, 8), :], sems.at[i]
            )
        )
        copies[i].start()

    @pl.when(late)
    def _():
        pltpu.make_async_copy(first_late, first_v, sems.at[2]).start()

    @pl.when(jnp.logical_not(late))
    def _():
        pltpu.make_async_copy(first, first_v, sems.at[2]).start()

    copies.append(pltpu.make_async_copy(first, first_v, sems.at[2]))
    copies.append(pltpu.make_async_copy(second, second_v, sems.at[3]))
    copies[3].start()
    for copy in copies:
        copy.wait()
    offset = start * LON - block * 8
    for i in range(3 * LON):
        masks[i:i + 1, :] = ocean_v[pl.ds(offset + i, 1), :].astype(jnp.float32)

    def run(slot, side, own_ref, out_ref, cross_ref):
        def load(base):
            return [None] * LON + [own_ref[own_rows(base, n), :] for n in range(LON)]

        def store(base, level, cross, far):
            for n in range(LON):
                out_ref[own_rows(base, n), :] = level[n]
                if far is not None:
                    cross_ref[cross_rows(cross, n), :] = far[n]

        advance(slot, side, courant_ref, times_ref, masks, load, store)

    for side in range(2):

        @pl.when(hemi == side)
        def _(side=side):
            run(0, side, first_v, out0, cross0)
            run(1, side, second_v, out1, cross1)


def halo_load(halo_ref):
    def load(base):
        return [halo_ref[own_rows(base, n), :] for n in range(LON)] + [None] * LON

    return load


def early_kernel(courant_ref, times_ref, masks_ref, halo_ref, own_ref, own_cross, out_ref, cross_ref):
    def store(base, level, cross, far):
        for n in range(LON):
            out_ref[own_rows(base, n), :] = own_ref[own_rows(base, n), :] + level[n]
            if far is not None:
                value = own_cross[cross_rows(cross, n), :]
                cross_ref[cross_rows(cross, n), :] = total(value, far[n])

    for side in range(2):

        @pl.when(lax.axis_index("hemi") == side)
        def _(side=side):
            advance(0, side, courant_ref, times_ref, masks_ref, halo_load(halo_ref), store)


def stage_rows(slot, hemi, base, n):
    j = base // NF + 12 * slot
    place = j - 6 if 6 <= j < 18 else (j + 6 if j < 6 else j - 18)
    forward = hemi if slot == 0 else 1 - hemi
    lon = LON - 1 - n if forward else n
    return pl.ds((base % NF) * 48 + place * LON + lon, 8, stride=48)


def behind_first(hemi, side):
    x = lax.rem(lax.axis_index("dev"), SIDE)
    return (hemi == side) & (x == (SIDE - 2 if side else 1))


def late_half(toward, courant_ref, times_ref, masks_ref, halo0, halo1, acc0, acc1, stage, cross_in,
              cross_out):
    hemi = lax.axis_index("hemi")
    rates = (courant_ref, times_ref, masks_ref)

    def keep(side, slot, acc):
        def store(base, level, cross, far):
            for n in range(LON):
                stage[stage_rows(slot, side, base, n), :] = acc[own_rows(base, n), :] + level[n]
                if far is not None:
                    value = cross_in[slot][cross_rows(cross, n), :]
                    cross_out[slot, cross_rows(cross, n), :] = total(value, far[n])

        return store

    for side in range(2):

        @pl.when(hemi == side)
        def _(side=side):
            advance(1, side, *rates, halo_load(halo1), keep(side, 1, acc1), (toward,))

        @pl.when(behind_first(hemi, side))
        def _(side=side):
            advance(0, side, *rates, halo_load(halo0), keep(side, 0, acc0), (toward,))

        @pl.when((hemi == side) & jnp.logical_not(behind_first(hemi, side)))
        def _(side=side):
            for i in range(6):
                for half in range(2):
                    base = (i + 6 * toward) * NF + half * 8
                    for n in range(LON):
                        stage[stage_rows(0, side, base, n), :] = acc0[own_rows(base, n), :]
            if toward:
                cross_out[0] = cross_in[0][...]


def toward_kernel(courant_ref, times_ref, masks_ref, halo0, halo1, acc0, acc1, cross0, cross1,
                  stage, cross_out):
    late_half(1, courant_ref, times_ref, masks_ref, halo0, halo1, acc0, acc1, stage,
              (cross0, cross1), cross_out)


def half_copies(stage, out, toward, sems):
    hemi = lax.axis_index("hemi")
    at = pl.multiple_of(48 * (hemi if toward else 1 - hemi), 8)
    copies = []
    for f in range(NF):
        copies.append(
            pltpu.make_async_copy(
                stage.at[pl.ds(48 * f, 48), :], out.at[pl.ds(96 * f + at, 48), :], sems.at[f]
            )
        )
    return copies


def away_kernel(courant_ref, times_ref, masks_ref, halo0, halo1, acc0, acc1, ready, stage, out, sems):
    copies = half_copies(ready, out, 1, sems)
    for copy in copies:
        copy.start()
    late_half(0, courant_ref, times_ref, masks_ref, halo0, halo1, acc0, acc1, stage, None, None)
    for copy in copies:
        copy.wait()


def join_kernel(stage, cross_ref, _, out, ready, sems):
    for side in range(2):

        @pl.when(lax.axis_index("hemi") == side)
        def _(side=side):
            for slot in range(2):
                for i in range(6):
                    for half in range(2):
                        base = (i + 6 * slot) * NF + half * 8
                        cross = i * NF + half * 8
                        for n in range(LON):
                            rows = stage_rows(slot, side, base, n)
                            ready[rows, :] = stage[rows, :] + cross_ref[1 - slot, cross_rows(cross, n), :]

    copies = half_copies(ready, out, 0, sems)
    for copy in copies:
        copy.start()
    for copy in copies:
        copy.wait()


SMEM = pl.BlockSpec(memory_space=pltpu.SMEM)
VMEM = pl.BlockSpec(memory_space=pltpu.VMEM)
HBM = pl.BlockSpec(memory_space=pltpu.HBM)


def params(mib=40):
    return pltpu.CompilerParams(vmem_limit_bytes=mib * MIB)


def cost(flops):
    return pl.CostEstimate(flops=int(flops), bytes_accessed=1000, transcendentals=0)


SOURCE_SCRATCH = [
    pltpu.VMEM((K * LON, LAT), jnp.float32),
    pltpu.VMEM((LON, LAT), jnp.float32),
    pltpu.VMEM((LON, LAT), jnp.int32),
    pltpu.VMEM((K,), jnp.float32),
    pltpu.VMEM((2 * K, K), jnp.int32),
    pltpu.VMEM((8, 2 * LAT), jnp.int32),
    pltpu.VMEM((LON * HALF, LAT), jnp.float32),
    pltpu.VMEM((LON * HALF, LAT), jnp.float32),
    pltpu.SemaphoreType.DMA((8,)),
    pltpu.VMEM((2 * K, 2 * K), jnp.bfloat16),
    pltpu.VMEM((K, 2 * K), jnp.bfloat16),
    pltpu.VMEM((K * LON, LAT), jnp.float32),
    pltpu.VMEM((2 * K, PTS), jnp.bfloat16),
    pltpu.VMEM((2 * K, PTS), jnp.float32),
    pltpu.VMEM((2 * K, PTS), jnp.bfloat16),
    pltpu.VMEM((K, PTS), jnp.float32),
    pltpu.VMEM((K, LAT), jnp.float32),
]


def local(spectrum, wind_speed, src_counts, ocean_mask, growth, quadruplet, courant, freq_counts):
    n_dev = lax.axis_size("dev")
    half_shape = jax.ShapeDtypeStruct((LON * HALF, LAT), jnp.float32)
    cross_shape = jax.ShapeDtypeStruct((LON * GROUP, LAT), jnp.float32)
    mask_shape = jax.ShapeDtypeStruct((3 * LON, 2 * LAT), jnp.float32)
    out_shape = jax.ShapeDtypeStruct((K * LON, LAT), jnp.float32)
    given = (
        spectrum.reshape(K * LON, LAT), wind_speed, src_counts, growth,
        quadruplet.reshape(2 * K, K), ocean_mask,
    )

    def source(late, *more, **aliases):
        return pl.pallas_call(
            functools.partial(source_kernel, late),
            out_shape=(half_shape, half_shape),
            in_specs=[HBM] * (6 + len(more)),
            out_specs=(HBM, HBM),
            scratch_shapes=SOURCE_SCRATCH,
            compiler_params=params(56),
            cost_estimate=cost(6e9),
            **aliases,
        )(*given, *more)

    first, second = source(False)

    axes = ("hemi", "dev")

    def pairs(back, keep):
        out = []
        for h in range(2):
            sign = -1 if h ^ back else 1
            for i in range(n_dev):
                source = h * n_dev + i
                end = SIDE - 1 if h else 0
                if keep(i % SIDE == end):
                    out.append((source, h * n_dev + (i + sign) % n_dev))
        return out

    def idle():
        out = []
        for h in range(2):
            for i in range(n_dev):
                x = i % SIDE if h == 0 else SIDE - 1 - i % SIDE
                if x > 1:
                    out.append((h * n_dev + i, h * n_dev + i))
        return out

    halo_first = lax.ppermute(first, axes, pairs(0, lambda late: not late))
    first_late, second = source(True, second, input_output_aliases={6: 1})
    halo_second = lax.ppermute(second, axes, pairs(1, lambda late: True))
    halo_late = lax.ppermute(first_late, axes, pairs(0, lambda late: late) + idle())

    out0, out1, cross0, cross1, masks = pl.pallas_call(
        own_kernel,
        out_shape=(half_shape, half_shape, cross_shape, cross_shape, mask_shape),
        in_specs=[SMEM] * 2 + [HBM] * 4,
        out_specs=(VMEM,) * 5,
        scratch_shapes=[
            pltpu.VMEM((LON * HALF, LAT), jnp.float32),
            pltpu.VMEM((LON * HALF, LAT), jnp.float32),
            pltpu.VMEM((16, 2 * LAT), jnp.int32),
            pltpu.SemaphoreType.DMA((4,)),
        ],
        compiler_params=params(),
        cost_estimate=cost(3e9),
    )(courant, freq_counts, ocean_mask, first, first_late, second)
    rates = (courant, freq_counts, masks)
    out0, cross0 = pl.pallas_call(
        early_kernel,
        out_shape=(half_shape, cross_shape),
        in_specs=[SMEM] * 2 + [VMEM] * 4,
        out_specs=(VMEM, VMEM),
        compiler_params=params(),
        cost_estimate=cost(1e9),
    )(*rates, halo_first, out0, cross0)
    late = (*rates, halo_late, halo_second, out0, out1)
    stage, cross = pl.pallas_call(
        toward_kernel,
        out_shape=(half_shape, jax.ShapeDtypeStruct((2, LON * GROUP, LAT), jnp.float32)),
        in_specs=[SMEM] * 2 + [VMEM] * 7,
        out_specs=(VMEM, VMEM),
        compiler_params=params(),
        cost_estimate=cost(1e9),
    )(*late, cross0, cross1)
    cross = lax.ppermute(cross, "hemi", [(0, 1), (1, 0)])
    stage, out = pl.pallas_call(
        away_kernel,
        out_shape=(half_shape, out_shape),
        in_specs=[SMEM] * 2 + [VMEM] * 6,
        out_specs=(VMEM, HBM),
        scratch_shapes=[pltpu.SemaphoreType.DMA((NF,))],
        compiler_params=params(),
        cost_estimate=cost(1e9),
    )(*late, stage)
    out = pl.pallas_call(
        join_kernel,
        out_shape=out_shape,
        in_specs=[VMEM, VMEM, HBM],
        out_specs=HBM,
        scratch_shapes=[
            pltpu.VMEM((LON * HALF, LAT), jnp.float32),
            pltpu.SemaphoreType.DMA((NF,)),
        ],
        input_output_aliases={2: 0},
        compiler_params=params(),
    )(stage, cross, out)
    return out.reshape(K, LON, LAT)


def solution(mesh):
    return jax.shard_map(
        local,
        mesh=mesh,
        in_specs=(
            P(None, "dev", "hemi"),
            P("dev", "hemi"),
            P("dev", "hemi"),
            P(),
            P(),
            P(),
            P(),
            P(),
        ),
        out_specs=P(None, "dev", "hemi"),
        check_vma=False,
    )
```

```python
import functools
import math

import jax
import jax.numpy as jnp
from jax import lax
from jax.experimental import pallas as pl
from jax.experimental.pallas import tpu as pltpu
from jax.sharding import PartitionSpec as P

ND = 24
NF = 16
K = ND * NF
LON = 4
LAT = 128
PTS = LON * LAT
SRC_MAX = 3
SPLIT = 2
GATHER_BLOCK = 128
SCATTER_BLOCK = 128
SUB_MAX = 4
HALF = K // 2
GROUP = 6 * NF
QUARTER = 6 * LON
coupling = 0.25
breaking = 0.5
spread = 0.7
MIB = 1024 * 1024
SIDE = 4


def direction(j, hemi):
    return lax.rem(18 + j + 12 * hemi, ND)


def split(value):
    high = value.astype(jnp.bfloat16)
    low = (value - high.astype(jnp.float32)).astype(jnp.bfloat16)
    return high, low


def role(hemi, dev):
    x = lax.rem(dev, SIDE)
    return (x == 0) & (hemi == 0) | (x == SIDE - 1) & (hemi == 1)


def source_terms(
    hemi, dev, ocean_ref, growth_ref, wind_ref, count_ref, quad_ref, spec_ref, waits, send,
    gather_m, scatter_m, energy, parts, paired, terms, moved, grow,
):
    nt = (((1,), (1,)), ((), ()))
    eye = (
        lax.broadcasted_iota(jnp.int32, (K, K), 0) == lax.broadcasted_iota(jnp.int32, (K, K), 1)
    ).astype(jnp.float32)
    eye_bf = eye.astype(jnp.bfloat16)
    waits["small"]()
    rest = jnp.broadcast_to(growth_ref[...].reshape(1, K), (LAT, K))
    column = None
    for _ in range(3):
        part = rest.astype(jnp.bfloat16)
        rest = rest - part.astype(jnp.float32)
        term = lax.dot_general(eye_bf, part, nt, preferred_element_type=jnp.float32)
        column = term if column is None else column + term
    grow[...] = column

    winds = []
    oceans = []
    counts = []
    for lon in range(LON):
        winds.append(wind_ref[lon:lon + 1, :])
        counts.append(count_ref[lon:lon + 1, :])
        row = ocean_ref[pl.ds(LON * lax.rem(dev, 2) + lon, 1), :].astype(jnp.float32)
        oceans.append(jnp.where(hemi == 0, row[:, :LAT], row[:, LAT:]))
    steps = [oceans[lon] / counts[lon].astype(jnp.float32) for lon in range(LON)]

    waits["quad"]()
    sides = []
    for side in range(2):
        rows = quad_ref[side * K:(side + 1) * K, :].astype(jnp.float32).astype(jnp.bfloat16)
        gather_m[side * K:(side + 1) * K, :K] = rows
        gather_m[side * K:(side + 1) * K, K:] = rows
        sides.append(rows)
    back = lax.dot_general(eye_bf, sides[0] + sides[1], nt, preferred_element_type=jnp.float32)
    back = (coupling * (back - 2.0 * eye)).astype(jnp.bfloat16)
    scatter_m[:, :K] = back
    scatter_m[:, K:] = back

    waits["spec"]()
    per = LON // SPLIT
    for part in range(SPLIT):
        for i in range(K // NF):
            for sub in range(per):
                lon = part * per + sub
                cols = slice(sub * LAT, (sub + 1) * LAT)
                value = spec_ref[pl.ds(i * NF * LON + lon, NF, stride=LON), :] * oceans[lon]
                energy[lon * K + i * NF:lon * K + (i + 1) * NF, :] = value
                high, low = split(value)
                parts[part, i * NF:(i + 1) * NF, cols] = high
                parts[part, K + i * NF:K + (i + 1) * NF, cols] = low

    def gather_rows(part, rows):
        def run():
            paired[part, rows, :] = jnp.dot(
                gather_m[rows, :], parts[part], preferred_element_type=jnp.float32
            )
        return run

    def scatter_rows(part, rows):
        def run():
            moved[part, rows, :] = jnp.dot(
                scatter_m[rows, :], terms[part], preferred_element_type=jnp.float32
            )
        return run

    def quad_rows(part, i):
        def run():
            at = slice(i * NF, (i + 1) * NF)
            below = slice(K + i * NF, K + (i + 1) * NF)
            for sub in range(per):
                lon = part * per + sub
                cols = slice(sub * LAT, (sub + 1) * LAT)
                value = energy[lon * K + i * NF:lon * K + (i + 1) * NF, :]
                plus = paired[part, at, cols]
                minus = paired[part, below, cols]
                term = value * (value * (plus + minus) - 2.0 * (plus * minus))
                high, low = split(term)
                terms[part, at, cols] = high
                terms[part, below, cols] = low
        return run

    def update_rows(part, i, cycle):
        def run():
            at = slice(i * NF, (i + 1) * NF)
            below = slice(K + i * NF, K + (i + 1) * NF)
            rate = grow[at, :]
            for sub in range(per):
                lon = part * per + sub
                cols = slice(sub * LAT, (sub + 1) * LAT)
                value = energy[lon * K + i * NF:lon * K + (i + 1) * NF, :]
                tendency = value * (rate * winds[lon] - breaking * value)
                tendency = tendency + moved[part, at, cols]
                value = jnp.where(cycle < counts[lon], value + steps[lon] * tendency, value)
                energy[lon * K + i * NF:lon * K + (i + 1) * NF, :] = value
                if cycle < SRC_MAX - 1:
                    high, low = split(value)
                    parts[part, at, cols] = high
                    parts[part, below, cols] = low
        return run

    def weave(dots, rows):
        per_dot = -(-len(rows) // max(len(dots), 1))
        for n in range(max(len(dots), 1)):
            for dot in dots[n:n + 1]:
                dot()
            for row in rows[n * per_dot:(n + 1) * per_dot]:
                row()

    def blocks(make, part, count, size):
        return [make(part, slice(n, n + size)) for n in range(0, count, size)]

    steps_of = K // NF
    weave(blocks(gather_rows, 0, 2 * K, GATHER_BLOCK), [])
    for cycle in range(SRC_MAX):
        weave(blocks(gather_rows, 1, 2 * K, GATHER_BLOCK), [quad_rows(0, i) for i in range(steps_of)])
        weave(blocks(scatter_rows, 0, K, SCATTER_BLOCK), [quad_rows(1, i) for i in range(steps_of)])
        weave(blocks(scatter_rows, 1, K, SCATTER_BLOCK), [update_rows(0, i, cycle) for i in range(steps_of)])
        if cycle < SRC_MAX - 1:
            weave(blocks(gather_rows, 0, 2 * K, GATHER_BLOCK), [update_rows(1, i, cycle) for i in range(steps_of)])
        else:
            for lon in range(per):
                send(lon)
            weave([], [update_rows(1, i, cycle) for i in range(steps_of)])
            for lon in range(per, LON):
                send(lon)


def source_kernel(late, spec, wind, count, growth, quad, ocean, *refs):
    first, second = refs[1:3] if late else refs[:2]
    scratch = refs[3:] if late else refs[2:]
    spec_v, wind_v, count_v, growth_v, quad_v, ocean_v, first_v, second_v, sems = scratch[:9]
    work = scratch[9:]
    hemi = lax.axis_index("hemi")
    dev = lax.axis_index("dev")
    mine = role(hemi, dev) if late else jnp.logical_not(role(hemi, dev))

    @pl.when(mine)
    def _():
        block = pl.multiple_of(dev // 2 * 8, 8)
        small = [
            pltpu.make_async_copy(growth, growth_v, sems.at[2]),
            pltpu.make_async_copy(wind, wind_v, sems.at[3]),
            pltpu.make_async_copy(count, count_v, sems.at[4]),
            pltpu.make_async_copy(ocean.at[pl.ds(block, 8), :], ocean_v, sems.at[5]),
        ]
        large = {
            "quad": pltpu.make_async_copy(quad, quad_v, sems.at[0]),
            "spec": pltpu.make_async_copy(spec, spec_v, sems.at[1]),
        }
        large["quad"].start()
        for copy in small:
            copy.start()
        large["spec"].start()

        def wait_small():
            for copy in small:
                copy.wait()

        waits = {"small": wait_small, "quad": large["quad"].wait, "spec": large["spec"].wait}
        outs = []

        def send(lon):
            for slot, (source, target) in enumerate(((first_v, first), (second_v, second))):
                forward = hemi if slot == 0 else 1 - hemi
                n = lon + forward * (LON - 1 - 2 * lon)
                rows = pl.ds(pl.multiple_of(n * HALF, HALF), HALF)
                for jj in range(12):
                    d = direction(jj + 12 * slot, hemi)
                    source[lon, jj * NF:(jj + 1) * NF, :] = work[2][pl.ds(lon * K + d, NF, stride=ND), :]
                copy = pltpu.make_async_copy(source.at[lon], target.at[rows, :], sems.at[6 + 2 * lon + slot])
                copy.start()
                outs.append(copy)

        source_terms(
            hemi, dev, ocean_v, growth_v, wind_v, count_v, quad_v, spec_v, waits, send, *work,
        )
        for copy in outs:
            copy.wait()


BATCH = (6, 3)


def fine(value, active):
    return value if active is None else jnp.where(active, value, 0.0)


def total(*terms):
    terms = [term for term in terms if term is not None]
    if not terms:
        return None
    out = terms[0]
    for term in terms[1:]:
        out = out + term
    return out


def times(rate, value):
    return None if value is None else rate * value


def advance(slot, hemi, courant_ref, times_ref, masks_ref, load, store, which=(1, 0)):
    forward = hemi if slot == 0 else 1 - hemi
    lanes = slice(hemi * LAT, (hemi + 1) * LAT)
    far_lanes = slice((1 - hemi) * LAT, (2 - hemi) * LAT)
    masks = []
    far_masks = []
    for n in range(-LON, LON):
        at = LON + (n if forward == 0 else LON - 1 - n)
        masks.append(jnp.broadcast_to(masks_ref[at:at + 1, lanes], (8, LAT)))
        far_masks.append(jnp.broadcast_to(masks_ref[at:at + 1, far_lanes], (8, LAT)))
    lane = lax.broadcasted_iota(jnp.int32, (8, LAT), 1)
    row8 = lax.broadcasted_iota(jnp.int32, (8, LAT), 0)
    rates = []
    for half in range(2):
        courant = jnp.zeros((8, LAT), jnp.float32)
        count = jnp.zeros((8, LAT), jnp.int32)
        for r in range(8):
            courant = jnp.where(row8 == r, courant_ref[half * 8 + r], courant)
            count = jnp.where(row8 == r, times_ref[half * 8 + r], count)
        rates.append((spread * courant, [None] + [count > t for t in range(1, SUB_MAX)]))
    for toward in which:
        up = hemi if toward == 0 else 1 - hemi
        shift = 1 if up else LAT - 1
        edge = lane == (0 if up else LAT - 1)
        batch = BATCH[toward]
        for half in range(2):
            speed, active = rates[half]
            for first in range(0, 6, batch):
                groups = []
                for i in range(first, first + batch):
                    jj = i + (6 * toward if slot == 0 else 6 * (1 - toward))
                    angle = 2.0 * math.pi * ((18 + jj + 12 * slot) % ND + 0.5) / ND
                    cx = speed * abs(math.cos(angle))
                    cy = speed * abs(math.sin(angle))
                    base = jj * NF + half * 8
                    cross = i * NF + half * 8
                    groups.append((base, cross, cx, cy, 1.0 - cx - cy, load(base), [None] * (2 * LON)))
                for t in range(SUB_MAX):
                    for n in range(2 * LON - 1, t, -1):
                        for base, cross, cx, cy, stay, level, far in groups:
                            rolled = None if level[n] is None else pltpu.roll(level[n], shift, 1)
                            south = None if rolled is None else jnp.where(edge, 0.0, rolled)
                            value = total(times(stay, level[n]), times(cx, level[n - 1]), times(cy, south))
                            if toward:
                                inflow = None
                                if far[n] is not None:
                                    inflow = jnp.where(edge, rolled, pltpu.roll(far[n], shift, 1))
                                elif rolled is not None:
                                    inflow = jnp.where(edge, rolled, 0.0)
                                other = total(times(stay, far[n]), times(cx, far[n - 1]), times(cy, inflow))
                                if other is not None:
                                    other = far_masks[n] * other
                                    if t:
                                        old = 0.0 if far[n] is None else far[n]
                                        other = jnp.where(active[t], other, old)
                                    far[n] = other
                            if value is not None:
                                value = masks[n] * value
                                if t:
                                    old = 0.0 if level[n] is None else level[n]
                                    value = jnp.where(active[t], value, old)
                                level[n] = value
                for base, cross, cx, cy, stay, level, far in groups:
                    store(base, level[LON:], cross, far[LON:] if toward else None)


def own_rows(base, n):
    return slice(n * HALF + base, n * HALF + base + 8)


def cross_rows(cross, n):
    return slice(n * GROUP + cross, n * GROUP + cross + 8)


def own_kernel(
    courant_ref, times_ref, ocean, first, first_late, second, out0, out1, cross0, cross1, masks,
    first_v, second_v, ocean_v, sems,
):
    hemi = lax.axis_index("hemi")
    dev = lax.axis_index("dev")
    n_dev = lax.axis_size("dev")
    late = role(hemi, dev)
    start = lax.rem(dev + n_dev - 1, n_dev)
    block = start // 2
    blocks = n_dev * LON // 8
    copies = []
    for i in range(2):
        at = pl.multiple_of(lax.rem(block + i, blocks) * 8, 8)
        copies.append(
            pltpu.make_async_copy(
                ocean.at[pl.ds(at, 8), :], ocean_v.at[pl.ds(8 * i, 8), :], sems.at[i]
            )
        )
        copies[i].start()

    @pl.when(late)
    def _():
        pltpu.make_async_copy(first_late, first_v, sems.at[2]).start()

    @pl.when(jnp.logical_not(late))
    def _():
        pltpu.make_async_copy(first, first_v, sems.at[2]).start()

    copies.append(pltpu.make_async_copy(first, first_v, sems.at[2]))
    copies.append(pltpu.make_async_copy(second, second_v, sems.at[3]))
    copies[3].start()
    for copy in copies:
        copy.wait()
    offset = start * LON - block * 8
    for i in range(3 * LON):
        masks[i:i + 1, :] = ocean_v[pl.ds(offset + i, 1), :].astype(jnp.float32)

    def run(slot, side, own_ref, out_ref, cross_ref):
        def load(base):
            return [None] * LON + [own_ref[own_rows(base, n), :] for n in range(LON)]

        def store(base, level, cross, far):
            for n in range(LON):
                out_ref[own_rows(base, n), :] = level[n]
                if far is not None:
                    cross_ref[cross_rows(cross, n), :] = far[n]

        advance(slot, side, courant_ref, times_ref, masks, load, store)

    for side in range(2):

        @pl.when(hemi == side)
        def _(side=side):
            run(0, side, first_v, out0, cross0)
            run(1, side, second_v, out1, cross1)


def halo_load(halo_ref, other_ref=None, other=None):
    def load(base):
        out = []
        for n in range(LON):
            value = halo_ref[own_rows(base, n), :]
            if other_ref is not None:
                value = jnp.where(other, other_ref[own_rows(base, n), :], value)
            out.append(value)
        return out + [None] * LON

    return load


def stage_rows(slot, hemi, base, n):
    i = base // NF % 6
    forward = hemi if slot == 0 else 1 - hemi
    lon = LON - 1 - n if forward else n
    return pl.ds((base % NF) * QUARTER + i * LON + lon, 8, stride=QUARTER)


def quarter_copy(slot, toward, stage, out, sem):
    hemi = lax.axis_index("hemi")
    part = slot if toward else 1 - slot
    at = pl.multiple_of(2 * QUARTER * (hemi if toward else 1 - hemi) + QUARTER * part, 8)
    return pltpu.make_async_copy(
        stage.reshape(NF, QUARTER, LAT), out.at[:, pl.ds(at, QUARTER), :], sem
    )


def group_bases(slot, toward):
    first = 6 * toward if slot == 0 else 6 * (1 - toward)
    return [(i * NF + half * 8 + first * NF, i * NF + half * 8) for i in range(6) for half in range(2)]


def add_halo(slot, toward, side, rates, load, acc, stage, cross_in=None, cross_out=None):
    def store(base, level, cross, far):
        for n in range(LON):
            rows = stage_rows(slot, side, base, n)
            stage[rows, :] = acc[own_rows(base, n), :] + level[n]
            if far is not None:
                value = cross_in[cross_rows(cross, n), :]
                cross_out[cross_rows(cross, n), :] = total(value, far[n])

    advance(slot, side, *rates, load, store, (toward,))


def behind_first(side):
    x = lax.rem(lax.axis_index("dev"), SIDE)
    return (lax.axis_index("hemi") == side) & (x == (SIDE - 2 if side else 1))


def toward_kernel(courant_ref, times_ref, masks_ref, halo0, halo1, halo_late, acc0, acc1, cross0,
                  cross1, _, ready0, ready1, cross_out):
    rates = (courant_ref, times_ref, masks_ref)
    behind = behind_first(0) | behind_first(1)
    for side in range(2):

        @pl.when(lax.axis_index("hemi") == side)
        def _(side=side):
            load = halo_load(halo0, halo_late, behind)
            add_halo(0, 1, side, rates, load, acc0, ready0, cross0, cross_out.at[0])
            add_halo(1, 1, side, rates, halo_load(halo1), acc1, ready1, cross1, cross_out.at[1])


def mark_kernel(*refs):
    refs[-1][...] = jnp.zeros((8, LAT), jnp.float32)


def away_kernel(courant_ref, times_ref, masks_ref, halo0, halo1, halo_late, acc0, acc1, ready0,
                ready1, stage0, stage1, out, sems):
    behind = behind_first(0) | behind_first(1)
    copies = [quarter_copy(0, 1, ready0, out, sems.at[0]), quarter_copy(1, 1, ready1, out, sems.at[1])]
    for copy in copies:
        copy.start()
    rates = (courant_ref, times_ref, masks_ref)
    for side in range(2):

        @pl.when(lax.axis_index("hemi") == side)
        def _(side=side):
            add_halo(0, 0, side, rates, halo_load(halo0, halo_late, behind), acc0, stage0)
            add_halo(1, 0, side, rates, halo_load(halo1), acc1, stage1)

    for copy in copies:
        copy.wait()


def join_kernel(stage0, stage1, cross, _, out, ready0, ready1, sems):
    copies = []
    for slot, stage, ready in ((0, stage0, ready0), (1, stage1, ready1)):
        for side in range(2):

            @pl.when(lax.axis_index("hemi") == side)
            def _(side=side):
                first = 6 * slot * NF
                for i in range(6):
                    for half in range(2):
                        at = i * NF + half * 8
                        for n in range(LON):
                            rows = stage_rows(slot, side, first + at, n)
                            ready[rows, :] = stage[rows, :] + cross[1 - slot, cross_rows(at, n), :]

        copies.append(quarter_copy(slot, 0, ready, out, sems.at[slot]))
        copies[slot].start()
    for copy in copies:
        copy.wait()


SMEM = pl.BlockSpec(memory_space=pltpu.SMEM)
VMEM = pl.BlockSpec(memory_space=pltpu.VMEM)
HBM = pl.BlockSpec(memory_space=pltpu.HBM)


def params(mib=40):
    return pltpu.CompilerParams(vmem_limit_bytes=int(mib * MIB))


def cost(flops):
    return pl.CostEstimate(flops=int(flops), bytes_accessed=1000, transcendentals=0)


SOURCE_SCRATCH = [
    pltpu.VMEM((K * LON, LAT), jnp.float32),
    pltpu.VMEM((LON, LAT), jnp.float32),
    pltpu.VMEM((LON, LAT), jnp.int32),
    pltpu.VMEM((K,), jnp.float32),
    pltpu.VMEM((2 * K, K), jnp.int32),
    pltpu.VMEM((8, 2 * LAT), jnp.int32),
    pltpu.VMEM((LON, HALF, LAT), jnp.float32),
    pltpu.VMEM((LON, HALF, LAT), jnp.float32),
    pltpu.SemaphoreType.DMA((6 + 2 * LON,)),
    pltpu.VMEM((2 * K, 2 * K), jnp.bfloat16),
    pltpu.VMEM((K, 2 * K), jnp.bfloat16),
    pltpu.VMEM((K * LON, LAT), jnp.float32),
    pltpu.VMEM((SPLIT, 2 * K, PTS // SPLIT), jnp.bfloat16),
    pltpu.VMEM((SPLIT, 2 * K, PTS // SPLIT), jnp.float32),
    pltpu.VMEM((SPLIT, 2 * K, PTS // SPLIT), jnp.bfloat16),
    pltpu.VMEM((SPLIT, K, PTS // SPLIT), jnp.float32),
    pltpu.VMEM((K, LAT), jnp.float32),
]


def local(spectrum, wind_speed, src_counts, ocean_mask, growth, quadruplet, courant, freq_counts):
    n_dev = lax.axis_size("dev")
    half_shape = jax.ShapeDtypeStruct((LON * HALF, LAT), jnp.float32)
    cross_shape = jax.ShapeDtypeStruct((LON * GROUP, LAT), jnp.float32)
    mask_shape = jax.ShapeDtypeStruct((3 * LON, 2 * LAT), jnp.float32)
    out_shape = jax.ShapeDtypeStruct((NF, ND * LON, LAT), jnp.float32)
    given = (
        spectrum.reshape(K * LON, LAT), wind_speed, src_counts, growth,
        quadruplet.reshape(2 * K, K), ocean_mask,
    )

    def source(late, *more, **aliases):
        return pl.pallas_call(
            functools.partial(source_kernel, late),
            out_shape=(half_shape, half_shape),
            in_specs=[HBM] * (6 + len(more)),
            out_specs=(HBM, HBM),
            scratch_shapes=SOURCE_SCRATCH,
            compiler_params=params(56),
            cost_estimate=cost(6e9),
            **aliases,
        )(*given, *more)

    first, second = source(False)

    axes = ("hemi", "dev")

    def pairs(back, keep):
        out = []
        for h in range(2):
            sign = -1 if h ^ back else 1
            for i in range(n_dev):
                source = h * n_dev + i
                end = SIDE - 1 if h else 0
                if keep(i % SIDE == end):
                    out.append((source, h * n_dev + (i + sign) % n_dev))
        return out

    def idle():
        out = []
        for h in range(2):
            for i in range(n_dev):
                x = i % SIDE if h == 0 else SIDE - 1 - i % SIDE
                if x > 1:
                    out.append((h * n_dev + i, h * n_dev + i))
        return out

    halo_first = lax.ppermute(first, axes, pairs(0, lambda late: not late))
    first_late, second = source(True, second, input_output_aliases={6: 1})
    halo_second = lax.ppermute(second, axes, pairs(1, lambda late: True))
    halo_late = lax.ppermute(first_late, axes, pairs(0, lambda late: late) + idle())

    out0, out1, cross0, cross1, masks = pl.pallas_call(
        own_kernel,
        out_shape=(half_shape, half_shape, cross_shape, cross_shape, mask_shape),
        in_specs=[SMEM] * 2 + [HBM] * 4,
        out_specs=(VMEM,) * 5,
        scratch_shapes=[
            pltpu.VMEM((LON * HALF, LAT), jnp.float32),
            pltpu.VMEM((LON * HALF, LAT), jnp.float32),
            pltpu.VMEM((16, 2 * LAT), jnp.int32),
            pltpu.SemaphoreType.DMA((4,)),
        ],
        compiler_params=params(52.6),
        cost_estimate=cost(3e9),
    )(courant, freq_counts, ocean_mask, first, first_late, second)
    rates = (courant, freq_counts, masks)
    quarter_shape = jax.ShapeDtypeStruct((NF * QUARTER, LAT), jnp.float32)

    def tail(kernel, outs, count, *operands, **more):
        return pl.pallas_call(
            kernel,
            out_shape=outs,
            in_specs=[SMEM] * 2 + [VMEM] * (1 + count),
            compiler_params=params(),
            cost_estimate=cost(1e9),
            **more,
        )(*rates, *operands)

    def mark(*values):
        return pl.pallas_call(
            mark_kernel,
            out_shape=jax.ShapeDtypeStruct((8, LAT), jnp.float32),
            in_specs=[VMEM] * len(values),
            out_specs=VMEM,
            compiler_params=params(),
            cost_estimate=cost(1e8),
        )(*values)

    order = mark(halo_first, out0)
    order = mark(halo_second, order)
    both_shape = jax.ShapeDtypeStruct((2, LON * GROUP, LAT), jnp.float32)
    halos = (halo_first, halo_second, halo_late, out0, out1)
    ready0, ready1, cross = tail(
        toward_kernel, (quarter_shape, quarter_shape, both_shape), 8, *halos, cross0, cross1, order,
        out_specs=(VMEM,) * 3,
    )
    cross = lax.ppermute(cross, "hemi", [(0, 1), (1, 0)])
    stage0, stage1, out = tail(
        away_kernel, (quarter_shape, quarter_shape, out_shape), 7, *halos, ready0, ready1,
        out_specs=(VMEM, VMEM, HBM), scratch_shapes=[pltpu.SemaphoreType.DMA((2,))],
    )
    out = pl.pallas_call(
        join_kernel,
        out_shape=out_shape,
        in_specs=[VMEM] * 3 + [HBM],
        out_specs=HBM,
        scratch_shapes=[
            pltpu.VMEM((NF * QUARTER, LAT), jnp.float32),
            pltpu.VMEM((NF * QUARTER, LAT), jnp.float32),
            pltpu.SemaphoreType.DMA((2,)),
        ],
        input_output_aliases={3: 0},
        compiler_params=params(),
    )(stage0, stage1, cross, out)
    return out.reshape(K, LON, LAT)


def solution(mesh):
    return jax.shard_map(
        local,
        mesh=mesh,
        in_specs=(
            P(None, "dev", "hemi"),
            P("dev", "hemi"),
            P("dev", "hemi"),
            P(),
            P(),
            P(),
            P(),
            P(),
        ),
        out_specs=P(None, "dev", "hemi"),
        check_vma=False,
    )
```

```python
import functools
import math

import jax
import jax.numpy as jnp
from jax import lax
from jax.experimental import pallas as pl
from jax.experimental.pallas import tpu as pltpu
from jax.sharding import PartitionSpec as P

ND = 24
NF = 16
K = ND * NF
LON = 4
LAT = 128
PTS = LON * LAT
SRC_MAX = 3
SPLIT = 2
GATHER_BLOCK = 128
SCATTER_BLOCK = 128
SUB_MAX = 4
HALF = K // 2
GROUP = 6 * NF
QUARTER = 6 * LON
coupling = 0.25
breaking = 0.5
spread = 0.7
MIB = 1024 * 1024


def direction(j, hemi):
    return lax.rem(18 + j + 12 * hemi, ND)


def split(value):
    high = value.astype(jnp.bfloat16)
    low = (value - high.astype(jnp.float32)).astype(jnp.bfloat16)
    return high, low


def source_terms(
    hemi, dev, ocean_ref, growth_ref, wind_ref, count_ref, quad_ref, spec_ref, waits, send,
    gather_m, scatter_m, energy, parts, paired, terms, moved, grow,
):
    nt = (((1,), (1,)), ((), ()))
    eye = (
        lax.broadcasted_iota(jnp.int32, (K, K), 0) == lax.broadcasted_iota(jnp.int32, (K, K), 1)
    ).astype(jnp.float32)
    eye_bf = eye.astype(jnp.bfloat16)
    waits["small"]()
    rest = jnp.broadcast_to(growth_ref[...].reshape(1, K), (LAT, K))
    column = None
    for _ in range(3):
        part = rest.astype(jnp.bfloat16)
        rest = rest - part.astype(jnp.float32)
        term = lax.dot_general(eye_bf, part, nt, preferred_element_type=jnp.float32)
        column = term if column is None else column + term
    grow[...] = column

    winds = []
    oceans = []
    counts = []
    for lon in range(LON):
        winds.append(wind_ref[lon:lon + 1, :])
        counts.append(count_ref[lon:lon + 1, :])
        row = ocean_ref[pl.ds(LON * lax.rem(dev, 2) + lon, 1), :].astype(jnp.float32)
        oceans.append(jnp.where(hemi == 0, row[:, :LAT], row[:, LAT:]))
    steps = [oceans[lon] / counts[lon].astype(jnp.float32) for lon in range(LON)]

    waits["quad"]()
    sides = []
    for side in range(2):
        rows = quad_ref[side * K:(side + 1) * K, :].astype(jnp.float32).astype(jnp.bfloat16)
        gather_m[side * K:(side + 1) * K, :K] = rows
        gather_m[side * K:(side + 1) * K, K:] = rows
        sides.append(rows)
    back = lax.dot_general(eye_bf, sides[0] + sides[1], nt, preferred_element_type=jnp.float32)
    back = (coupling * (back - 2.0 * eye)).astype(jnp.bfloat16)
    scatter_m[:, :K] = back
    scatter_m[:, K:] = back

    waits["spec"]()
    per = LON // SPLIT
    for part in range(SPLIT):
        for i in range(K // NF):
            for sub in range(per):
                lon = part * per + sub
                cols = slice(sub * LAT, (sub + 1) * LAT)
                value = spec_ref[pl.ds(i * NF * LON + lon, NF, stride=LON), :] * oceans[lon]
                energy[lon * K + i * NF:lon * K + (i + 1) * NF, :] = value
                high, low = split(value)
                parts[part, i * NF:(i + 1) * NF, cols] = high
                parts[part, K + i * NF:K + (i + 1) * NF, cols] = low

    def gather_rows(part, rows):
        def run():
            paired[part, rows, :] = jnp.dot(
                gather_m[rows, :], parts[part], preferred_element_type=jnp.float32
            )
        return run

    def scatter_rows(part, rows):
        def run():
            moved[part, rows, :] = jnp.dot(
                scatter_m[rows, :], terms[part], preferred_element_type=jnp.float32
            )
        return run

    def quad_rows(part, i):
        def run():
            at = slice(i * NF, (i + 1) * NF)
            below = slice(K + i * NF, K + (i + 1) * NF)
            for sub in range(per):
                lon = part * per + sub
                cols = slice(sub * LAT, (sub + 1) * LAT)
                value = energy[lon * K + i * NF:lon * K + (i + 1) * NF, :]
                plus = paired[part, at, cols]
                minus = paired[part, below, cols]
                term = value * (value * (plus + minus) - 2.0 * (plus * minus))
                high, low = split(term)
                terms[part, at, cols] = high
                terms[part, below, cols] = low
        return run

    def update_rows(part, i, cycle):
        def run():
            at = slice(i * NF, (i + 1) * NF)
            below = slice(K + i * NF, K + (i + 1) * NF)
            rate = grow[at, :]
            for sub in range(per):
                lon = part * per + sub
                cols = slice(sub * LAT, (sub + 1) * LAT)
                value = energy[lon * K + i * NF:lon * K + (i + 1) * NF, :]
                tendency = value * (rate * winds[lon] - breaking * value)
                tendency = tendency + moved[part, at, cols]
                value = jnp.where(cycle < counts[lon], value + steps[lon] * tendency, value)
                energy[lon * K + i * NF:lon * K + (i + 1) * NF, :] = value
                if cycle < SRC_MAX - 1:
                    high, low = split(value)
                    parts[part, at, cols] = high
                    parts[part, below, cols] = low
        return run

    def weave(dots, rows):
        per_dot = -(-len(rows) // max(len(dots), 1))
        for n in range(max(len(dots), 1)):
            for dot in dots[n:n + 1]:
                dot()
            for row in rows[n * per_dot:(n + 1) * per_dot]:
                row()

    def blocks(make, part, count, size):
        return [make(part, slice(n, n + size)) for n in range(0, count, size)]

    steps_of = K // NF
    weave(blocks(gather_rows, 0, 2 * K, GATHER_BLOCK), [])
    for cycle in range(SRC_MAX):
        weave(blocks(gather_rows, 1, 2 * K, GATHER_BLOCK), [quad_rows(0, i) for i in range(steps_of)])
        weave(blocks(scatter_rows, 0, K, SCATTER_BLOCK), [quad_rows(1, i) for i in range(steps_of)])
        weave(blocks(scatter_rows, 1, K, SCATTER_BLOCK), [update_rows(0, i, cycle) for i in range(steps_of)])
        if cycle < SRC_MAX - 1:
            weave(blocks(gather_rows, 0, 2 * K, GATHER_BLOCK), [update_rows(1, i, cycle) for i in range(steps_of)])
        else:
            for lon in range(per):
                send(lon)
            weave([], [update_rows(1, i, cycle) for i in range(steps_of)])
            for lon in range(per, LON):
                send(lon)


def source_kernel(
    spec, wind, count, growth, quad, ocean, east, west,
    spec_v, wind_v, count_v, growth_v, quad_v, ocean_v, first_v, second_v, sems, *work,
):
    hemi = lax.axis_index("hemi")
    dev = lax.axis_index("dev")
    block = pl.multiple_of(dev // 2 * 8, 8)
    small = [
        pltpu.make_async_copy(growth, growth_v, sems.at[2]),
        pltpu.make_async_copy(wind, wind_v, sems.at[3]),
        pltpu.make_async_copy(count, count_v, sems.at[4]),
        pltpu.make_async_copy(ocean.at[pl.ds(block, 8), :], ocean_v, sems.at[5]),
    ]
    large = {
        "quad": pltpu.make_async_copy(quad, quad_v, sems.at[0]),
        "spec": pltpu.make_async_copy(spec, spec_v, sems.at[1]),
    }
    large["quad"].start()
    for copy in small:
        copy.start()
    large["spec"].start()

    def wait_small():
        for copy in small:
            copy.wait()

    waits = {"small": wait_small, "quad": large["quad"].wait, "spec": large["spec"].wait}
    outs = []

    def send(lon):
        for slot, source in enumerate((first_v, second_v)):
            forward = hemi if slot == 0 else 1 - hemi
            n = lon + forward * (LON - 1 - 2 * lon)
            rows = pl.ds(pl.multiple_of(n * HALF, HALF), HALF)
            for jj in range(12):
                d = direction(jj + 12 * slot, hemi)
                source[lon, jj * NF:(jj + 1) * NF, :] = work[2][pl.ds(lon * K + d, NF, stride=ND), :]
            for side in range(2):
                copy = pltpu.make_async_copy(
                    source.at[lon], (east, west)[slot ^ side].at[rows, :], sems.at[6 + 2 * lon + slot]
                )
                pl.when(hemi == side)(copy.start)
            outs.append(copy)

    source_terms(
        hemi, dev, ocean_v, growth_v, wind_v, count_v, quad_v, spec_v, waits, send, *work,
    )
    for copy in outs:
        copy.wait()


BATCH = (6, 3)


def fine(value, active):
    return value if active is None else jnp.where(active, value, 0.0)


def total(*terms):
    terms = [term for term in terms if term is not None]
    if not terms:
        return None
    out = terms[0]
    for term in terms[1:]:
        out = out + term
    return out


def times(rate, value):
    return None if value is None else rate * value


def advance(slot, hemi, courant_ref, times_ref, masks_ref, load, store, which=(1, 0)):
    forward = hemi if slot == 0 else 1 - hemi
    lanes = slice(hemi * LAT, (hemi + 1) * LAT)
    far_lanes = slice((1 - hemi) * LAT, (2 - hemi) * LAT)
    masks = []
    far_masks = []
    for n in range(-LON, LON):
        at = LON + (n if forward == 0 else LON - 1 - n)
        masks.append(jnp.broadcast_to(masks_ref[at:at + 1, lanes], (8, LAT)))
        far_masks.append(jnp.broadcast_to(masks_ref[at:at + 1, far_lanes], (8, LAT)))
    lane = lax.broadcasted_iota(jnp.int32, (8, LAT), 1)
    row8 = lax.broadcasted_iota(jnp.int32, (8, LAT), 0)
    rates = []
    for half in range(2):
        courant = jnp.zeros((8, LAT), jnp.float32)
        count = jnp.zeros((8, LAT), jnp.int32)
        for r in range(8):
            courant = jnp.where(row8 == r, courant_ref[half * 8 + r], courant)
            count = jnp.where(row8 == r, times_ref[half * 8 + r], count)
        rates.append((spread * courant, [None] + [count > t for t in range(1, SUB_MAX)]))
    for toward in which:
        up = hemi if toward == 0 else 1 - hemi
        shift = 1 if up else LAT - 1
        edge = lane == (0 if up else LAT - 1)
        batch = BATCH[toward]
        for half in range(2):
            speed, active = rates[half]
            for first in range(0, 6, batch):
                groups = []
                for i in range(first, first + batch):
                    jj = i + (6 * toward if slot == 0 else 6 * (1 - toward))
                    angle = 2.0 * math.pi * ((18 + jj + 12 * slot) % ND + 0.5) / ND
                    cx = speed * abs(math.cos(angle))
                    cy = speed * abs(math.sin(angle))
                    base = jj * NF + half * 8
                    cross = i * NF + half * 8
                    groups.append((base, cross, cx, cy, 1.0 - cx - cy, load(base), [None] * (2 * LON)))
                for t in range(SUB_MAX):
                    for n in range(2 * LON - 1, t, -1):
                        for base, cross, cx, cy, stay, level, far in groups:
                            rolled = None if level[n] is None else pltpu.roll(level[n], shift, 1)
                            south = None if rolled is None else jnp.where(edge, 0.0, rolled)
                            value = total(times(stay, level[n]), times(cx, level[n - 1]), times(cy, south))
                            if toward:
                                inflow = None
                                if far[n] is not None:
                                    inflow = jnp.where(edge, rolled, pltpu.roll(far[n], shift, 1))
                                elif rolled is not None:
                                    inflow = jnp.where(edge, rolled, 0.0)
                                other = total(times(stay, far[n]), times(cx, far[n - 1]), times(cy, inflow))
                                if other is not None:
                                    other = far_masks[n] * other
                                    if t:
                                        old = 0.0 if far[n] is None else far[n]
                                        other = jnp.where(active[t], other, old)
                                    far[n] = other
                            if value is not None:
                                value = masks[n] * value
                                if t:
                                    old = 0.0 if level[n] is None else level[n]
                                    value = jnp.where(active[t], value, old)
                                level[n] = value
                for base, cross, cx, cy, stay, level, far in groups:
                    store(base, level[LON:], cross, far[LON:] if toward else None)


def own_rows(base, n):
    return slice(n * HALF + base, n * HALF + base + 8)


def cross_rows(cross, n):
    return slice(n * GROUP + cross, n * GROUP + cross + 8)


def own_kernel(
    courant_ref, times_ref, ocean, east, west, out0, out1, cross0, cross1, masks,
    first_v, second_v, ocean_v, sems,
):
    hemi = lax.axis_index("hemi")
    dev = lax.axis_index("dev")
    n_dev = lax.axis_size("dev")
    start = lax.rem(dev + n_dev - 1, n_dev)
    block = start // 2
    blocks = n_dev * LON // 8
    copies = []
    for i in range(2):
        at = pl.multiple_of(lax.rem(block + i, blocks) * 8, 8)
        copies.append(
            pltpu.make_async_copy(
                ocean.at[pl.ds(at, 8), :], ocean_v.at[pl.ds(8 * i, 8), :], sems.at[i]
            )
        )
        copies[i].start()

    for side in range(2):

        @pl.when(hemi == side)
        def _(side=side):
            pltpu.make_async_copy((east, west)[side], first_v, sems.at[2]).start()
            pltpu.make_async_copy((west, east)[side], second_v, sems.at[3]).start()

    copies.append(pltpu.make_async_copy(east, first_v, sems.at[2]))
    copies.append(pltpu.make_async_copy(west, second_v, sems.at[3]))
    for copy in copies:
        copy.wait()
    offset = start * LON - block * 8
    for i in range(3 * LON):
        masks[i:i + 1, :] = ocean_v[pl.ds(offset + i, 1), :].astype(jnp.float32)

    def run(slot, side, own_ref, out_ref, cross_ref):
        def load(base):
            return [None] * LON + [own_ref[own_rows(base, n), :] for n in range(LON)]

        def store(base, level, cross, far):
            for n in range(LON):
                out_ref[own_rows(base, n), :] = level[n]
                if far is not None:
                    cross_ref[cross_rows(cross, n), :] = far[n]

        advance(slot, side, courant_ref, times_ref, masks, load, store)

    for side in range(2):

        @pl.when(hemi == side)
        def _(side=side):
            run(0, side, first_v, out0, cross0)
            run(1, side, second_v, out1, cross1)


def halo_load(halo_ref):
    def load(base):
        return [halo_ref[own_rows(base, n), :] for n in range(LON)] + [None] * LON

    return load


def stage_rows(slot, hemi, base, n):
    i = base // NF % 6
    forward = hemi if slot == 0 else 1 - hemi
    lon = LON - 1 - n if forward else n
    return pl.ds((base % NF) * QUARTER + i * LON + lon, 8, stride=QUARTER)


def quarter_copy(slot, toward, stage, out, sem):
    hemi = lax.axis_index("hemi")
    part = slot if toward else 1 - slot
    at = pl.multiple_of(2 * QUARTER * (hemi if toward else 1 - hemi) + QUARTER * part, 8)
    return pltpu.make_async_copy(
        stage.reshape(NF, QUARTER, LAT), out.at[:, pl.ds(at, QUARTER), :], sem
    )


def group_bases(slot, toward):
    first = 6 * toward if slot == 0 else 6 * (1 - toward)
    return [(i * NF + half * 8 + first * NF, i * NF + half * 8) for i in range(6) for half in range(2)]


def add_halo(slot, toward, side, rates, load, acc, stage, cross_in=None, cross_out=None):
    def store(base, level, cross, far):
        for n in range(LON):
            rows = stage_rows(slot, side, base, n)
            stage[rows, :] = acc[own_rows(base, n), :] + level[n]
            if far is not None:
                value = cross_in[cross_rows(cross, n), :]
                cross_out[cross_rows(cross, n), :] = total(value, far[n])

    advance(slot, side, *rates, load, store, (toward,))


def toward_kernel(courant_ref, times_ref, masks_ref, east, west, acc0, acc1, cross0, cross1, _,
                  ready0, ready1, cross_out):
    rates = (courant_ref, times_ref, masks_ref)
    for side in range(2):

        @pl.when(lax.axis_index("hemi") == side)
        def _(side=side):
            halo0, halo1 = (east, west) if side == 0 else (west, east)
            add_halo(0, 1, side, rates, halo_load(halo0), acc0, ready0, cross0, cross_out.at[0])
            add_halo(1, 1, side, rates, halo_load(halo1), acc1, ready1, cross1, cross_out.at[1])


def mark_kernel(*refs):
    refs[-1][...] = jnp.zeros((8, LAT), jnp.float32)


def away_kernel(courant_ref, times_ref, masks_ref, east, west, acc0, acc1, ready0, ready1,
                stage0, stage1, out, sems):
    copies = [quarter_copy(0, 1, ready0, out, sems.at[0]), quarter_copy(1, 1, ready1, out, sems.at[1])]
    for copy in copies:
        copy.start()
    rates = (courant_ref, times_ref, masks_ref)
    for side in range(2):

        @pl.when(lax.axis_index("hemi") == side)
        def _(side=side):
            halo0, halo1 = (east, west) if side == 0 else (west, east)
            add_halo(0, 0, side, rates, halo_load(halo0), acc0, stage0)
            add_halo(1, 0, side, rates, halo_load(halo1), acc1, stage1)

    for copy in copies:
        copy.wait()


def join_kernel(stage0, stage1, cross, _, out, ready0, ready1, sems):
    copies = []
    for slot, stage, ready in ((0, stage0, ready0), (1, stage1, ready1)):
        for side in range(2):

            @pl.when(lax.axis_index("hemi") == side)
            def _(side=side):
                first = 6 * slot * NF
                for i in range(6):
                    for half in range(2):
                        at = i * NF + half * 8
                        for n in range(LON):
                            rows = stage_rows(slot, side, first + at, n)
                            ready[rows, :] = stage[rows, :] + cross[1 - slot, cross_rows(at, n), :]

        copies.append(quarter_copy(slot, 0, ready, out, sems.at[slot]))
        copies[slot].start()
    for copy in copies:
        copy.wait()


SMEM = pl.BlockSpec(memory_space=pltpu.SMEM)
VMEM = pl.BlockSpec(memory_space=pltpu.VMEM)
HBM = pl.BlockSpec(memory_space=pltpu.HBM)


def params(mib=40):
    return pltpu.CompilerParams(vmem_limit_bytes=int(mib * MIB))


def cost(flops):
    return pl.CostEstimate(flops=int(flops), bytes_accessed=1000, transcendentals=0)


SOURCE_SCRATCH = [
    pltpu.VMEM((K * LON, LAT), jnp.float32),
    pltpu.VMEM((LON, LAT), jnp.float32),
    pltpu.VMEM((LON, LAT), jnp.int32),
    pltpu.VMEM((K,), jnp.float32),
    pltpu.VMEM((2 * K, K), jnp.int32),
    pltpu.VMEM((8, 2 * LAT), jnp.int32),
    pltpu.VMEM((LON, HALF, LAT), jnp.float32),
    pltpu.VMEM((LON, HALF, LAT), jnp.float32),
    pltpu.SemaphoreType.DMA((6 + 2 * LON,)),
    pltpu.VMEM((2 * K, 2 * K), jnp.bfloat16),
    pltpu.VMEM((K, 2 * K), jnp.bfloat16),
    pltpu.VMEM((K * LON, LAT), jnp.float32),
    pltpu.VMEM((SPLIT, 2 * K, PTS // SPLIT), jnp.bfloat16),
    pltpu.VMEM((SPLIT, 2 * K, PTS // SPLIT), jnp.float32),
    pltpu.VMEM((SPLIT, 2 * K, PTS // SPLIT), jnp.bfloat16),
    pltpu.VMEM((SPLIT, K, PTS // SPLIT), jnp.float32),
    pltpu.VMEM((K, LAT), jnp.float32),
]


def local(spectrum, wind_speed, src_counts, ocean_mask, growth, quadruplet, courant, freq_counts):
    n_dev = lax.axis_size("dev")
    half_shape = jax.ShapeDtypeStruct((LON * HALF, LAT), jnp.float32)
    cross_shape = jax.ShapeDtypeStruct((LON * GROUP, LAT), jnp.float32)
    mask_shape = jax.ShapeDtypeStruct((3 * LON, 2 * LAT), jnp.float32)
    out_shape = jax.ShapeDtypeStruct((NF, ND * LON, LAT), jnp.float32)
    given = (
        spectrum.reshape(K * LON, LAT), wind_speed, src_counts, growth,
        quadruplet.reshape(2 * K, K), ocean_mask,
    )

    east, west = pl.pallas_call(
        source_kernel,
        out_shape=(half_shape, half_shape),
        in_specs=[HBM] * 6,
        out_specs=(HBM, HBM),
        scratch_shapes=SOURCE_SCRATCH,
        compiler_params=params(56),
        cost_estimate=cost(6e9),
    )(*given)

    ring = range(n_dev)
    halo_east = lax.ppermute(east, "dev", [(i, (i + 1) % n_dev) for i in ring])
    halo_west = lax.ppermute(west, "dev", [(i, (i - 1) % n_dev) for i in ring])

    out0, out1, cross0, cross1, masks = pl.pallas_call(
        own_kernel,
        out_shape=(half_shape, half_shape, cross_shape, cross_shape, mask_shape),
        in_specs=[SMEM] * 2 + [HBM] * 3,
        out_specs=(VMEM,) * 5,
        scratch_shapes=[
            pltpu.VMEM((LON * HALF, LAT), jnp.float32),
            pltpu.VMEM((LON * HALF, LAT), jnp.float32),
            pltpu.VMEM((16, 2 * LAT), jnp.int32),
            pltpu.SemaphoreType.DMA((4,)),
        ],
        compiler_params=params(52.6),
        cost_estimate=cost(3e9),
    )(courant, freq_counts, ocean_mask, east, west)
    rates = (courant, freq_counts, masks)
    quarter_shape = jax.ShapeDtypeStruct((NF * QUARTER, LAT), jnp.float32)

    def tail(kernel, outs, count, *operands, **more):
        return pl.pallas_call(
            kernel,
            out_shape=outs,
            in_specs=[SMEM] * 2 + [VMEM] * (1 + count),
            compiler_params=params(),
            cost_estimate=cost(1e9),
            **more,
        )(*rates, *operands)

    def mark(*values):
        return pl.pallas_call(
            mark_kernel,
            out_shape=jax.ShapeDtypeStruct((8, LAT), jnp.float32),
            in_specs=[VMEM] * len(values),
            out_specs=VMEM,
            compiler_params=params(),
            cost_estimate=cost(1e8),
        )(*values)

    order = mark(halo_east, out0)
    both_shape = jax.ShapeDtypeStruct((2, LON * GROUP, LAT), jnp.float32)
    halos = (halo_east, halo_west, out0, out1)
    ready0, ready1, cross = tail(
        toward_kernel, (quarter_shape, quarter_shape, both_shape), 7, *halos, cross0, cross1, order,
        out_specs=(VMEM,) * 3,
    )
    cross = lax.ppermute(cross, "hemi", [(0, 1), (1, 0)])
    stage0, stage1, out = tail(
        away_kernel, (quarter_shape, quarter_shape, out_shape), 6, *halos, ready0, ready1,
        out_specs=(VMEM, VMEM, HBM), scratch_shapes=[pltpu.SemaphoreType.DMA((2,))],
    )
    out = pl.pallas_call(
        join_kernel,
        out_shape=out_shape,
        in_specs=[VMEM] * 3 + [HBM],
        out_specs=HBM,
        scratch_shapes=[
            pltpu.VMEM((NF * QUARTER, LAT), jnp.float32),
            pltpu.VMEM((NF * QUARTER, LAT), jnp.float32),
            pltpu.SemaphoreType.DMA((2,)),
        ],
        input_output_aliases={3: 0},
        compiler_params=params(),
    )(stage0, stage1, cross, out)
    return out.reshape(K, LON, LAT)


def solution(mesh):
    return jax.shard_map(
        local,
        mesh=mesh,
        in_specs=(
            P(None, "dev", "hemi"),
            P("dev", "hemi"),
            P("dev", "hemi"),
            P(),
            P(),
            P(),
            P(),
            P(),
        ),
        out_specs=P(None, "dev", "hemi"),
        check_vma=False,
    )
```

```python
import functools
import math

import jax
import jax.numpy as jnp
from jax import lax
from jax.experimental import pallas as pl
from jax.experimental.pallas import tpu as pltpu
from jax.sharding import PartitionSpec as P

ND = 24
NF = 16
K = ND * NF
LON = 4
LAT = 128
PTS = LON * LAT
SRC_MAX = 3
SPLIT = 2
GATHER_BLOCK = 128
SCATTER_BLOCK = 128
SUB_MAX = 4
HALF = K // 2
GROUP = 6 * NF
QUARTER = 6 * LON
coupling = 0.25
breaking = 0.5
spread = 0.7
MIB = 1024 * 1024


def direction(j, hemi):
    return lax.rem(18 + j + 12 * hemi, ND)


def split(value):
    high = value.astype(jnp.bfloat16)
    low = (value - high.astype(jnp.float32)).astype(jnp.bfloat16)
    return high, low


def source_terms(
    hemi, dev, ocean_ref, growth_ref, wind_ref, count_ref, quad_ref, spec_ref, waits, send,
    gather_m, scatter_m, energy, parts, paired, terms, moved, grow,
):
    nt = (((1,), (1,)), ((), ()))
    eye = (
        lax.broadcasted_iota(jnp.int32, (K, K), 0) == lax.broadcasted_iota(jnp.int32, (K, K), 1)
    ).astype(jnp.float32)
    eye_bf = eye.astype(jnp.bfloat16)
    waits["small"]()
    rest = jnp.broadcast_to(growth_ref[...].reshape(1, K), (LAT, K))
    column = None
    for _ in range(3):
        part = rest.astype(jnp.bfloat16)
        rest = rest - part.astype(jnp.float32)
        term = lax.dot_general(eye_bf, part, nt, preferred_element_type=jnp.float32)
        column = term if column is None else column + term
    grow[...] = column

    winds = []
    oceans = []
    counts = []
    for lon in range(LON):
        winds.append(wind_ref[lon:lon + 1, :])
        counts.append(count_ref[lon:lon + 1, :])
        row = ocean_ref[pl.ds(LON * lax.rem(dev, 2) + lon, 1), :].astype(jnp.float32)
        oceans.append(jnp.where(hemi == 0, row[:, :LAT], row[:, LAT:]))
    steps = [oceans[lon] / counts[lon].astype(jnp.float32) for lon in range(LON)]

    waits["quad"]()
    sides = []
    for side in range(2):
        rows = quad_ref[side * K:(side + 1) * K, :].astype(jnp.float32).astype(jnp.bfloat16)
        gather_m[side * K:(side + 1) * K, :K] = rows
        gather_m[side * K:(side + 1) * K, K:] = rows
        sides.append(rows)
    back = lax.dot_general(eye_bf, sides[0] + sides[1], nt, preferred_element_type=jnp.float32)
    back = (coupling * (back - 2.0 * eye)).astype(jnp.bfloat16)
    scatter_m[:, :K] = back
    scatter_m[:, K:] = back

    waits["spec"]()
    per = LON // SPLIT
    for part in range(SPLIT):
        for i in range(K // NF):
            for sub in range(per):
                lon = part * per + sub
                cols = slice(sub * LAT, (sub + 1) * LAT)
                value = spec_ref[pl.ds(i * NF * LON + lon, NF, stride=LON), :] * oceans[lon]
                energy[lon * K + i * NF:lon * K + (i + 1) * NF, :] = value
                high, low = split(value)
                parts[part, i * NF:(i + 1) * NF, cols] = high
                parts[part, K + i * NF:K + (i + 1) * NF, cols] = low

    def gather_rows(part, rows):
        def run():
            paired[part, rows, :] = jnp.dot(
                gather_m[rows, :], parts[part], preferred_element_type=jnp.float32
            )
        return run

    def scatter_rows(part, rows):
        def run():
            moved[part, rows, :] = jnp.dot(
                scatter_m[rows, :], terms[part], preferred_element_type=jnp.float32
            )
        return run

    def quad_rows(part, i):
        def run():
            at = slice(i * NF, (i + 1) * NF)
            below = slice(K + i * NF, K + (i + 1) * NF)
            for sub in range(per):
                lon = part * per + sub
                cols = slice(sub * LAT, (sub + 1) * LAT)
                value = energy[lon * K + i * NF:lon * K + (i + 1) * NF, :]
                plus = paired[part, at, cols]
                minus = paired[part, below, cols]
                term = value * (value * (plus + minus) - 2.0 * (plus * minus))
                high, low = split(term)
                terms[part, at, cols] = high
                terms[part, below, cols] = low
        return run

    def update_rows(part, i, cycle):
        def run():
            at = slice(i * NF, (i + 1) * NF)
            below = slice(K + i * NF, K + (i + 1) * NF)
            rate = grow[at, :]
            for sub in range(per):
                lon = part * per + sub
                cols = slice(sub * LAT, (sub + 1) * LAT)
                value = energy[lon * K + i * NF:lon * K + (i + 1) * NF, :]
                tendency = value * (rate * winds[lon] - breaking * value)
                tendency = tendency + moved[part, at, cols]
                value = jnp.where(cycle < counts[lon], value + steps[lon] * tendency, value)
                energy[lon * K + i * NF:lon * K + (i + 1) * NF, :] = value
                if cycle < SRC_MAX - 1:
                    high, low = split(value)
                    parts[part, at, cols] = high
                    parts[part, below, cols] = low
        return run

    def weave(dots, rows):
        per_dot = -(-len(rows) // max(len(dots), 1))
        for n in range(max(len(dots), 1)):
            for dot in dots[n:n + 1]:
                dot()
            for row in rows[n * per_dot:(n + 1) * per_dot]:
                row()

    def blocks(make, part, count, size):
        return [make(part, slice(n, n + size)) for n in range(0, count, size)]

    steps_of = K // NF
    weave(blocks(gather_rows, 0, 2 * K, GATHER_BLOCK), [])
    for cycle in range(SRC_MAX):
        weave(blocks(gather_rows, 1, 2 * K, GATHER_BLOCK), [quad_rows(0, i) for i in range(steps_of)])
        weave(blocks(scatter_rows, 0, K, SCATTER_BLOCK), [quad_rows(1, i) for i in range(steps_of)])
        weave(blocks(scatter_rows, 1, K, SCATTER_BLOCK), [update_rows(0, i, cycle) for i in range(steps_of)])
        if cycle < SRC_MAX - 1:
            weave(blocks(gather_rows, 0, 2 * K, GATHER_BLOCK), [update_rows(1, i, cycle) for i in range(steps_of)])
        else:
            for lon in range(per):
                send(lon)
            weave([], [update_rows(1, i, cycle) for i in range(steps_of)])
            for lon in range(per, LON):
                send(lon)


def source_kernel(
    spec, wind, count, growth, quad, ocean, east, west,
    spec_v, wind_v, count_v, growth_v, quad_v, ocean_v, first_v, second_v, sems, *work,
):
    hemi = lax.axis_index("hemi")
    dev = lax.axis_index("dev")
    block = pl.multiple_of(dev // 2 * 8, 8)
    small = [
        pltpu.make_async_copy(growth, growth_v, sems.at[2]),
        pltpu.make_async_copy(wind, wind_v, sems.at[3]),
        pltpu.make_async_copy(count, count_v, sems.at[4]),
        pltpu.make_async_copy(ocean.at[pl.ds(block, 8), :], ocean_v, sems.at[5]),
    ]
    large = {
        "quad": pltpu.make_async_copy(quad, quad_v, sems.at[0]),
        "spec": pltpu.make_async_copy(spec, spec_v, sems.at[1]),
    }
    large["quad"].start()
    for copy in small:
        copy.start()
    large["spec"].start()

    def wait_small():
        for copy in small:
            copy.wait()

    waits = {"small": wait_small, "quad": large["quad"].wait, "spec": large["spec"].wait}
    outs = []

    def send(lon):
        for slot, source in enumerate((first_v, second_v)):
            forward = hemi if slot == 0 else 1 - hemi
            n = lon + forward * (LON - 1 - 2 * lon)
            rows = pl.ds(pl.multiple_of(n * HALF, HALF), HALF)
            for jj in range(12):
                d = direction(jj + 12 * slot, hemi)
                source[lon, jj * NF:(jj + 1) * NF, :] = work[2][pl.ds(lon * K + d, NF, stride=ND), :]
            for side in range(2):
                copy = pltpu.make_async_copy(
                    source.at[lon], (east, west)[slot ^ side].at[rows, :], sems.at[6 + 2 * lon + slot]
                )
                pl.when(hemi == side)(copy.start)
            outs.append(copy)

    source_terms(
        hemi, dev, ocean_v, growth_v, wind_v, count_v, quad_v, spec_v, waits, send, *work,
    )
    for copy in outs:
        copy.wait()


BATCH = (6, 6)


def fine(value, active):
    return value if active is None else jnp.where(active, value, 0.0)


def total(*terms):
    terms = [term for term in terms if term is not None]
    if not terms:
        return None
    out = terms[0]
    for term in terms[1:]:
        out = out + term
    return out


def times(rate, value):
    return None if value is None else rate * value


def advance(slot, hemi, courant_ref, times_ref, masks_ref, load, store, which=(1, 0)):
    forward = hemi if slot == 0 else 1 - hemi
    lanes = slice(hemi * LAT, (hemi + 1) * LAT)
    far_lanes = slice((1 - hemi) * LAT, (2 - hemi) * LAT)
    masks = []
    far_masks = []
    for n in range(-LON, LON):
        at = LON + (n if forward == 0 else LON - 1 - n)
        masks.append(jnp.broadcast_to(masks_ref[at:at + 1, lanes], (8, LAT)))
        far_masks.append(jnp.broadcast_to(masks_ref[at:at + 1, far_lanes], (8, LAT)))
    lane = lax.broadcasted_iota(jnp.int32, (8, LAT), 1)
    row8 = lax.broadcasted_iota(jnp.int32, (8, LAT), 0)
    rates = []
    for half in range(2):
        courant = jnp.zeros((8, LAT), jnp.float32)
        count = jnp.zeros((8, LAT), jnp.int32)
        for r in range(8):
            courant = jnp.where(row8 == r, courant_ref[half * 8 + r], courant)
            count = jnp.where(row8 == r, times_ref[half * 8 + r], count)
        rates.append((spread * courant, [None] + [count > t for t in range(1, SUB_MAX)]))
    for toward in which:
        up = hemi if toward == 0 else 1 - hemi
        shift = 1 if up else LAT - 1
        edge = lane == (0 if up else LAT - 1)
        batch = BATCH[toward]
        for half in range(2):
            speed, active = rates[half]
            for first in range(0, 6, batch):
                groups = []
                for i in range(first, first + batch):
                    jj = i + (6 * toward if slot == 0 else 6 * (1 - toward))
                    angle = 2.0 * math.pi * ((18 + jj + 12 * slot) % ND + 0.5) / ND
                    cx = speed * abs(math.cos(angle))
                    cy = speed * abs(math.sin(angle))
                    base = jj * NF + half * 8
                    cross = i * NF + half * 8
                    groups.append((base, cross, cx, cy, 1.0 - cx - cy, load(base), [None] * (2 * LON)))
                for t in range(SUB_MAX):
                    for n in range(2 * LON - 1, t, -1):
                        for base, cross, cx, cy, stay, level, far in groups:
                            rolled = None if level[n] is None else pltpu.roll(level[n], shift, 1)
                            south = None if rolled is None else jnp.where(edge, 0.0, rolled)
                            value = total(times(stay, level[n]), times(cx, level[n - 1]), times(cy, south))
                            if toward:
                                inflow = None
                                if far[n] is not None:
                                    inflow = jnp.where(edge, rolled, pltpu.roll(far[n], shift, 1))
                                elif rolled is not None:
                                    inflow = jnp.where(edge, rolled, 0.0)
                                other = total(times(stay, far[n]), times(cx, far[n - 1]), times(cy, inflow))
                                if other is not None:
                                    other = far_masks[n] * other
                                    if t:
                                        old = 0.0 if far[n] is None else far[n]
                                        other = jnp.where(active[t], other, old)
                                    far[n] = other
                            if value is not None:
                                value = masks[n] * value
                                if t:
                                    old = 0.0 if level[n] is None else level[n]
                                    value = jnp.where(active[t], value, old)
                                level[n] = value
                for base, cross, cx, cy, stay, level, far in groups:
                    store(base, level[LON:], cross, far[LON:] if toward else None)


def own_rows(base, n):
    return slice(n * HALF + base, n * HALF + base + 8)


def cross_rows(cross, n):
    return slice(n * GROUP + cross, n * GROUP + cross + 8)


def own_kernel(
    courant_ref, times_ref, ocean, east, west, out0, out1, cross0, cross1, masks,
    first_v, second_v, ocean_v, sems,
):
    hemi = lax.axis_index("hemi")
    dev = lax.axis_index("dev")
    n_dev = lax.axis_size("dev")
    start = lax.rem(dev + n_dev - 1, n_dev)
    block = start // 2
    blocks = n_dev * LON // 8
    copies = []
    for i in range(2):
        at = pl.multiple_of(lax.rem(block + i, blocks) * 8, 8)
        copies.append(
            pltpu.make_async_copy(
                ocean.at[pl.ds(at, 8), :], ocean_v.at[pl.ds(8 * i, 8), :], sems.at[i]
            )
        )
        copies[i].start()

    for side in range(2):

        @pl.when(hemi == side)
        def _(side=side):
            pltpu.make_async_copy((east, west)[side], first_v, sems.at[2]).start()
            pltpu.make_async_copy((west, east)[side], second_v, sems.at[3]).start()

    copies.append(pltpu.make_async_copy(east, first_v, sems.at[2]))
    copies.append(pltpu.make_async_copy(west, second_v, sems.at[3]))
    for copy in copies:
        copy.wait()
    offset = start * LON - block * 8
    for i in range(3 * LON):
        masks[i:i + 1, :] = ocean_v[pl.ds(offset + i, 1), :].astype(jnp.float32)

    def run(slot, side, own_ref, out_ref, cross_ref):
        def load(base):
            return [None] * LON + [own_ref[own_rows(base, n), :] for n in range(LON)]

        def store(base, level, cross, far):
            for n in range(LON):
                out_ref[own_rows(base, n), :] = level[n]
                if far is not None:
                    cross_ref[cross_rows(cross, n), :] = far[n]

        advance(slot, side, courant_ref, times_ref, masks, load, store)

    for side in range(2):

        @pl.when(hemi == side)
        def _(side=side):
            run(0, side, first_v, out0, cross0)
            run(1, side, second_v, out1, cross1)


def halo_load(halo_ref):
    def load(base):
        return [halo_ref[own_rows(base, n), :] for n in range(LON)] + [None] * LON

    return load


def stage_rows(slot, hemi, base, n):
    i = base // NF % 6
    forward = hemi if slot == 0 else 1 - hemi
    lon = LON - 1 - n if forward else n
    return pl.ds((base % NF) * QUARTER + i * LON + lon, 8, stride=QUARTER)


def quarter_copy(slot, toward, stage, out, sem):
    hemi = lax.axis_index("hemi")
    part = slot if toward else 1 - slot
    at = pl.multiple_of(2 * QUARTER * (hemi if toward else 1 - hemi) + QUARTER * part, 8)
    return pltpu.make_async_copy(
        stage.reshape(NF, QUARTER, LAT), out.at[:, pl.ds(at, QUARTER), :], sem
    )


def group_bases(slot, toward):
    first = 6 * toward if slot == 0 else 6 * (1 - toward)
    return [(i * NF + half * 8 + first * NF, i * NF + half * 8) for i in range(6) for half in range(2)]


def add_halo(slot, toward, side, rates, load, acc, stage, cross_in=None, cross_out=None):
    def store(base, level, cross, far):
        for n in range(LON):
            rows = stage_rows(slot, side, base, n)
            stage[rows, :] = acc[own_rows(base, n), :] + level[n]
            if far is not None:
                value = cross_in[cross_rows(cross, n), :]
                cross_out[cross_rows(cross, n), :] = total(value, far[n])

    advance(slot, side, *rates, load, store, (toward,))


def toward_kernel(courant_ref, times_ref, masks_ref, east, west, acc0, acc1, cross0, cross1, _,
                  ready0, ready1, cross_out):
    rates = (courant_ref, times_ref, masks_ref)
    for side in range(2):

        @pl.when(lax.axis_index("hemi") == side)
        def _(side=side):
            halo0, halo1 = (east, west) if side == 0 else (west, east)
            add_halo(0, 1, side, rates, halo_load(halo0), acc0, ready0, cross0, cross_out.at[0])
            add_halo(1, 1, side, rates, halo_load(halo1), acc1, ready1, cross1, cross_out.at[1])


def mark_kernel(*refs):
    refs[-1][...] = jnp.zeros((8, LAT), jnp.float32)


def away_kernel(courant_ref, times_ref, masks_ref, east, west, acc0, acc1, ready0, ready1,
                stage0, stage1, out, sems):
    copies = [quarter_copy(0, 1, ready0, out, sems.at[0]), quarter_copy(1, 1, ready1, out, sems.at[1])]
    for copy in copies:
        copy.start()
    rates = (courant_ref, times_ref, masks_ref)
    for side in range(2):

        @pl.when(lax.axis_index("hemi") == side)
        def _(side=side):
            halo0, halo1 = (east, west) if side == 0 else (west, east)
            add_halo(0, 0, side, rates, halo_load(halo0), acc0, stage0)
            add_halo(1, 0, side, rates, halo_load(halo1), acc1, stage1)

    for copy in copies:
        copy.wait()


def join_kernel(stage0, stage1, cross, _, out, ready0, ready1, sems):
    copies = []
    for slot, stage, ready in ((0, stage0, ready0), (1, stage1, ready1)):
        for side in range(2):

            @pl.when(lax.axis_index("hemi") == side)
            def _(side=side):
                first = 6 * slot * NF
                for i in range(6):
                    for half in range(2):
                        at = i * NF + half * 8
                        for n in range(LON):
                            rows = stage_rows(slot, side, first + at, n)
                            ready[rows, :] = stage[rows, :] + cross[1 - slot, cross_rows(at, n), :]

        copies.append(quarter_copy(slot, 0, ready, out, sems.at[slot]))
        copies[slot].start()
    for copy in copies:
        copy.wait()


SMEM = pl.BlockSpec(memory_space=pltpu.SMEM)
VMEM = pl.BlockSpec(memory_space=pltpu.VMEM)
HBM = pl.BlockSpec(memory_space=pltpu.HBM)


def params(mib=40):
    return pltpu.CompilerParams(vmem_limit_bytes=int(mib * MIB))


def cost(flops):
    return pl.CostEstimate(flops=int(flops), bytes_accessed=1000, transcendentals=0)


SOURCE_SCRATCH = [
    pltpu.VMEM((K * LON, LAT), jnp.float32),
    pltpu.VMEM((LON, LAT), jnp.float32),
    pltpu.VMEM((LON, LAT), jnp.int32),
    pltpu.VMEM((K,), jnp.float32),
    pltpu.VMEM((2 * K, K), jnp.int32),
    pltpu.VMEM((8, 2 * LAT), jnp.int32),
    pltpu.VMEM((LON, HALF, LAT), jnp.float32),
    pltpu.VMEM((LON, HALF, LAT), jnp.float32),
    pltpu.SemaphoreType.DMA((6 + 2 * LON,)),
    pltpu.VMEM((2 * K, 2 * K), jnp.bfloat16),
    pltpu.VMEM((K, 2 * K), jnp.bfloat16),
    pltpu.VMEM((K * LON, LAT), jnp.float32),
    pltpu.VMEM((SPLIT, 2 * K, PTS // SPLIT), jnp.bfloat16),
    pltpu.VMEM((SPLIT, 2 * K, PTS // SPLIT), jnp.float32),
    pltpu.VMEM((SPLIT, 2 * K, PTS // SPLIT), jnp.bfloat16),
    pltpu.VMEM((SPLIT, K, PTS // SPLIT), jnp.float32),
    pltpu.VMEM((K, LAT), jnp.float32),
]


def local(spectrum, wind_speed, src_counts, ocean_mask, growth, quadruplet, courant, freq_counts):
    n_dev = lax.axis_size("dev")
    half_shape = jax.ShapeDtypeStruct((LON * HALF, LAT), jnp.float32)
    cross_shape = jax.ShapeDtypeStruct((LON * GROUP, LAT), jnp.float32)
    mask_shape = jax.ShapeDtypeStruct((3 * LON, 2 * LAT), jnp.float32)
    out_shape = jax.ShapeDtypeStruct((NF, ND * LON, LAT), jnp.float32)
    given = (
        spectrum.reshape(K * LON, LAT), wind_speed, src_counts, growth,
        quadruplet.reshape(2 * K, K), ocean_mask,
    )

    east, west = pl.pallas_call(
        source_kernel,
        out_shape=(half_shape, half_shape),
        in_specs=[HBM] * 6,
        out_specs=(HBM, HBM),
        scratch_shapes=SOURCE_SCRATCH,
        compiler_params=params(56),
        cost_estimate=cost(6e9),
    )(*given)

    ring = range(n_dev)
    halo_east = lax.ppermute(east, "dev", [(i, (i + 1) % n_dev) for i in ring])
    halo_west = lax.ppermute(west, "dev", [(i, (i - 1) % n_dev) for i in ring])

    out0, out1, cross0, cross1, masks = pl.pallas_call(
        own_kernel,
        out_shape=(half_shape, half_shape, cross_shape, cross_shape, mask_shape),
        in_specs=[SMEM] * 2 + [HBM] * 3,
        out_specs=(VMEM,) * 5,
        scratch_shapes=[
            pltpu.VMEM((LON * HALF, LAT), jnp.float32),
            pltpu.VMEM((LON * HALF, LAT), jnp.float32),
            pltpu.VMEM((16, 2 * LAT), jnp.int32),
            pltpu.SemaphoreType.DMA((4,)),
        ],
        compiler_params=params(52.6),
        cost_estimate=cost(3e9),
    )(courant, freq_counts, ocean_mask, east, west)
    rates = (courant, freq_counts, masks)
    quarter_shape = jax.ShapeDtypeStruct((NF * QUARTER, LAT), jnp.float32)

    def tail(kernel, outs, count, *operands, **more):
        return pl.pallas_call(
            kernel,
            out_shape=outs,
            in_specs=[SMEM] * 2 + [VMEM] * (1 + count),
            compiler_params=params(),
            cost_estimate=cost(1e9),
            **more,
        )(*rates, *operands)

    def mark(*values):
        return pl.pallas_call(
            mark_kernel,
            out_shape=jax.ShapeDtypeStruct((8, LAT), jnp.float32),
            in_specs=[VMEM] * len(values),
            out_specs=VMEM,
            compiler_params=params(),
            cost_estimate=cost(1e8),
        )(*values)

    order = mark(halo_east, out0)
    both_shape = jax.ShapeDtypeStruct((2, LON * GROUP, LAT), jnp.float32)
    halos = (halo_east, halo_west, out0, out1)
    ready0, ready1, cross = tail(
        toward_kernel, (quarter_shape, quarter_shape, both_shape), 7, *halos, cross0, cross1, order,
        out_specs=(VMEM,) * 3,
    )
    cross = lax.ppermute(cross, "hemi", [(0, 1), (1, 0)])
    stage0, stage1, out = tail(
        away_kernel, (quarter_shape, quarter_shape, out_shape), 6, *halos, ready0, ready1,
        out_specs=(VMEM, VMEM, HBM), scratch_shapes=[pltpu.SemaphoreType.DMA((2,))],
    )
    out = pl.pallas_call(
        join_kernel,
        out_shape=out_shape,
        in_specs=[VMEM] * 3 + [HBM],
        out_specs=HBM,
        scratch_shapes=[
            pltpu.VMEM((NF * QUARTER, LAT), jnp.float32),
            pltpu.VMEM((NF * QUARTER, LAT), jnp.float32),
            pltpu.SemaphoreType.DMA((2,)),
        ],
        input_output_aliases={3: 0},
        compiler_params=params(),
    )(stage0, stage1, cross, out)
    return out.reshape(K, LON, LAT)


def solution(mesh):
    return jax.shard_map(
        local,
        mesh=mesh,
        in_specs=(
            P(None, "dev", "hemi"),
            P("dev", "hemi"),
            P("dev", "hemi"),
            P(),
            P(),
            P(),
            P(),
            P(),
        ),
        out_specs=P(None, "dev", "hemi"),
        check_vma=False,
    )
```

```python
import functools
import math

import jax
import jax.numpy as jnp
from jax import lax
from jax.experimental import pallas as pl
from jax.experimental.pallas import tpu as pltpu
from jax.sharding import PartitionSpec as P

ND = 24
NF = 16
K = ND * NF
LON = 4
LAT = 128
PTS = LON * LAT
SRC_MAX = 3
SPLIT = 2
GATHER_BLOCK = 128
SCATTER_BLOCK = 128
SUB_MAX = 4
HALF = K // 2
GROUP = 6 * NF
QUARTER = 6 * LON
coupling = 0.25
breaking = 0.5
spread = 0.7
MIB = 1024 * 1024


def direction(j, hemi):
    return lax.rem(18 + j + 12 * hemi, ND)


def split(value):
    high = value.astype(jnp.bfloat16)
    low = (value - high.astype(jnp.float32)).astype(jnp.bfloat16)
    return high, low


def source_terms(
    hemi, dev, ocean_ref, growth_ref, wind_ref, count_ref, quad_ref, spec_ref, waits, send,
    gather_m, scatter_m, energy, parts, paired, terms, moved, grow,
):
    nt = (((1,), (1,)), ((), ()))
    eye = (
        lax.broadcasted_iota(jnp.int32, (K, K), 0) == lax.broadcasted_iota(jnp.int32, (K, K), 1)
    ).astype(jnp.float32)
    eye_bf = eye.astype(jnp.bfloat16)
    waits["small"]()
    rest = jnp.broadcast_to(growth_ref[...].reshape(1, K), (LAT, K))
    column = None
    for _ in range(3):
        part = rest.astype(jnp.bfloat16)
        rest = rest - part.astype(jnp.float32)
        term = lax.dot_general(eye_bf, part, nt, preferred_element_type=jnp.float32)
        column = term if column is None else column + term
    grow[...] = column

    winds = []
    oceans = []
    counts = []
    for lon in range(LON):
        winds.append(wind_ref[lon:lon + 1, :])
        counts.append(count_ref[lon:lon + 1, :])
        row = ocean_ref[pl.ds(LON * lax.rem(dev, 2) + lon, 1), :].astype(jnp.float32)
        oceans.append(jnp.where(hemi == 0, row[:, :LAT], row[:, LAT:]))
    steps = [oceans[lon] / counts[lon].astype(jnp.float32) for lon in range(LON)]

    waits["quad"]()
    sides = []
    for side in range(2):
        rows = quad_ref[side * K:(side + 1) * K, :].astype(jnp.float32).astype(jnp.bfloat16)
        gather_m[side * K:(side + 1) * K, :K] = rows
        gather_m[side * K:(side + 1) * K, K:] = rows
        sides.append(rows)
    back = lax.dot_general(eye_bf, sides[0] + sides[1], nt, preferred_element_type=jnp.float32)
    back = (coupling * (back - 2.0 * eye)).astype(jnp.bfloat16)
    scatter_m[:, :K] = back
    scatter_m[:, K:] = back

    waits["spec"]()
    per = LON // SPLIT
    for part in range(SPLIT):
        for i in range(K // NF):
            for sub in range(per):
                lon = part * per + sub
                cols = slice(sub * LAT, (sub + 1) * LAT)
                value = spec_ref[pl.ds(i * NF * LON + lon, NF, stride=LON), :] * oceans[lon]
                energy[lon * K + i * NF:lon * K + (i + 1) * NF, :] = value
                high, low = split(value)
                parts[part, i * NF:(i + 1) * NF, cols] = high
                parts[part, K + i * NF:K + (i + 1) * NF, cols] = low

    def gather_rows(part, rows):
        def run():
            paired[part, rows, :] = jnp.dot(
                gather_m[rows, :], parts[part], preferred_element_type=jnp.float32
            )
        return run

    def scatter_rows(part, rows):
        def run():
            moved[part, rows, :] = jnp.dot(
                scatter_m[rows, :], terms[part], preferred_element_type=jnp.float32
            )
        return run

    def quad_rows(part, i):
        def run():
            at = slice(i * NF, (i + 1) * NF)
            below = slice(K + i * NF, K + (i + 1) * NF)
            for sub in range(per):
                lon = part * per + sub
                cols = slice(sub * LAT, (sub + 1) * LAT)
                value = energy[lon * K + i * NF:lon * K + (i + 1) * NF, :]
                plus = paired[part, at, cols]
                minus = paired[part, below, cols]
                term = value * (value * (plus + minus) - 2.0 * (plus * minus))
                high, low = split(term)
                terms[part, at, cols] = high
                terms[part, below, cols] = low
        return run

    def update_rows(part, i, cycle):
        def run():
            at = slice(i * NF, (i + 1) * NF)
            below = slice(K + i * NF, K + (i + 1) * NF)
            rate = grow[at, :]
            for sub in range(per):
                lon = part * per + sub
                cols = slice(sub * LAT, (sub + 1) * LAT)
                value = energy[lon * K + i * NF:lon * K + (i + 1) * NF, :]
                tendency = value * (rate * winds[lon] - breaking * value)
                tendency = tendency + moved[part, at, cols]
                value = jnp.where(cycle < counts[lon], value + steps[lon] * tendency, value)
                energy[lon * K + i * NF:lon * K + (i + 1) * NF, :] = value
                if cycle < SRC_MAX - 1:
                    high, low = split(value)
                    parts[part, at, cols] = high
                    parts[part, below, cols] = low
        return run

    def weave(dots, rows):
        per_dot = -(-len(rows) // max(len(dots), 1))
        for n in range(max(len(dots), 1)):
            for dot in dots[n:n + 1]:
                dot()
            for row in rows[n * per_dot:(n + 1) * per_dot]:
                row()

    def blocks(make, part, count, size):
        return [make(part, slice(n, n + size)) for n in range(0, count, size)]

    steps_of = K // NF
    weave(blocks(gather_rows, 0, 2 * K, GATHER_BLOCK), [])
    for cycle in range(SRC_MAX):
        weave(blocks(gather_rows, 1, 2 * K, GATHER_BLOCK), [quad_rows(0, i) for i in range(steps_of)])
        weave(blocks(scatter_rows, 0, K, SCATTER_BLOCK), [quad_rows(1, i) for i in range(steps_of)])
        weave(blocks(scatter_rows, 1, K, SCATTER_BLOCK), [update_rows(0, i, cycle) for i in range(steps_of)])
        if cycle < SRC_MAX - 1:
            weave(blocks(gather_rows, 0, 2 * K, GATHER_BLOCK), [update_rows(1, i, cycle) for i in range(steps_of)])
        else:
            for lon in range(per):
                send(lon)
            weave([], [update_rows(1, i, cycle) for i in range(steps_of)])
            for lon in range(per, LON):
                send(lon)


def source_kernel(
    spec, wind, count, growth, quad, ocean, east, west,
    spec_v, wind_v, count_v, growth_v, quad_v, ocean_v, first_v, second_v, sems, *work,
):
    hemi = lax.axis_index("hemi")
    dev = lax.axis_index("dev")
    block = pl.multiple_of(dev // 2 * 8, 8)
    small = [
        pltpu.make_async_copy(growth, growth_v, sems.at[2]),
        pltpu.make_async_copy(wind, wind_v, sems.at[3]),
        pltpu.make_async_copy(count, count_v, sems.at[4]),
        pltpu.make_async_copy(ocean.at[pl.ds(block, 8), :], ocean_v, sems.at[5]),
    ]
    large = {
        "quad": pltpu.make_async_copy(quad, quad_v, sems.at[0]),
        "spec": pltpu.make_async_copy(spec, spec_v, sems.at[1]),
    }
    large["quad"].start()
    for copy in small:
        copy.start()
    large["spec"].start()

    def wait_small():
        for copy in small:
            copy.wait()

    waits = {"small": wait_small, "quad": large["quad"].wait, "spec": large["spec"].wait}
    outs = []

    def send(lon):
        for slot, source in enumerate((first_v, second_v)):
            forward = hemi if slot == 0 else 1 - hemi
            n = lon + forward * (LON - 1 - 2 * lon)
            rows = pl.ds(pl.multiple_of(n * HALF, HALF), HALF)
            for jj in range(12):
                d = direction(jj + 12 * slot, hemi)
                source[lon, jj * NF:(jj + 1) * NF, :] = work[2][pl.ds(lon * K + d, NF, stride=ND), :]
            for side in range(2):
                copy = pltpu.make_async_copy(
                    source.at[lon], (east, west)[slot ^ side].at[rows, :], sems.at[6 + 2 * lon + slot]
                )
                pl.when(hemi == side)(copy.start)
            outs.append(copy)

    source_terms(
        hemi, dev, ocean_v, growth_v, wind_v, count_v, quad_v, spec_v, waits, send, *work,
    )
    for copy in outs:
        copy.wait()


BATCH = (12, 6)


def fine(value, active):
    return value if active is None else jnp.where(active, value, 0.0)


def total(*terms):
    terms = [term for term in terms if term is not None]
    if not terms:
        return None
    out = terms[0]
    for term in terms[1:]:
        out = out + term
    return out


def times(rate, value):
    return None if value is None else rate * value


def advance(slot, hemi, courant_ref, times_ref, masks_ref, load, store, which=(1, 0)):
    forward = hemi if slot == 0 else 1 - hemi
    lanes = slice(hemi * LAT, (hemi + 1) * LAT)
    far_lanes = slice((1 - hemi) * LAT, (2 - hemi) * LAT)
    masks = []
    far_masks = []
    for n in range(-LON, LON):
        at = LON + (n if forward == 0 else LON - 1 - n)
        masks.append(jnp.broadcast_to(masks_ref[at:at + 1, lanes], (8, LAT)))
        far_masks.append(jnp.broadcast_to(masks_ref[at:at + 1, far_lanes], (8, LAT)))
    lane = lax.broadcasted_iota(jnp.int32, (8, LAT), 1)
    row8 = lax.broadcasted_iota(jnp.int32, (8, LAT), 0)
    rates = []
    for half in range(2):
        courant = jnp.zeros((8, LAT), jnp.float32)
        count = jnp.zeros((8, LAT), jnp.int32)
        for r in range(8):
            courant = jnp.where(row8 == r, courant_ref[half * 8 + r], courant)
            count = jnp.where(row8 == r, times_ref[half * 8 + r], count)
        rates.append((spread * courant, [None] + [count > t for t in range(1, SUB_MAX)]))
    for toward in which:
        up = hemi if toward == 0 else 1 - hemi
        shift = 1 if up else LAT - 1
        edge = lane == (0 if up else LAT - 1)
        batch = BATCH[toward]
        both = [(half, i) for half in range(2) for i in range(6)]
        for first in range(0, 12, batch):
            groups = []
            for half, i in both[first:first + batch]:
                speed, active = rates[half]
                jj = i + (6 * toward if slot == 0 else 6 * (1 - toward))
                angle = 2.0 * math.pi * ((18 + jj + 12 * slot) % ND + 0.5) / ND
                cx = speed * abs(math.cos(angle))
                cy = speed * abs(math.sin(angle))
                base = jj * NF + half * 8
                cross = i * NF + half * 8
                groups.append((base, cross, cx, cy, 1.0 - cx - cy, load(base), [None] * (2 * LON), active))
            for t in range(SUB_MAX):
                for n in range(2 * LON - 1, t, -1):
                    for base, cross, cx, cy, stay, level, far, active in groups:
                        rolled = None if level[n] is None else pltpu.roll(level[n], shift, 1)
                        south = None if rolled is None else jnp.where(edge, 0.0, rolled)
                        value = total(times(stay, level[n]), times(cx, level[n - 1]), times(cy, south))
                        if toward:
                            inflow = None
                            if far[n] is not None:
                                inflow = jnp.where(edge, rolled, pltpu.roll(far[n], shift, 1))
                            elif rolled is not None:
                                inflow = jnp.where(edge, rolled, 0.0)
                            other = total(times(stay, far[n]), times(cx, far[n - 1]), times(cy, inflow))
                            if other is not None:
                                other = far_masks[n] * other
                                if t:
                                    old = 0.0 if far[n] is None else far[n]
                                    other = jnp.where(active[t], other, old)
                                far[n] = other
                        if value is not None:
                            value = masks[n] * value
                            if t:
                                old = 0.0 if level[n] is None else level[n]
                                value = jnp.where(active[t], value, old)
                            level[n] = value
            for base, cross, cx, cy, stay, level, far, active in groups:
                store(base, level[LON:], cross, far[LON:] if toward else None)


def own_rows(base, n):
    return slice(n * HALF + base, n * HALF + base + 8)


def cross_rows(cross, n):
    return slice(n * GROUP + cross, n * GROUP + cross + 8)


def own_kernel(
    courant_ref, times_ref, ocean, east, west, out0, out1, cross0, cross1, masks,
    first_v, second_v, ocean_v, sems,
):
    hemi = lax.axis_index("hemi")
    dev = lax.axis_index("dev")
    n_dev = lax.axis_size("dev")
    start = lax.rem(dev + n_dev - 1, n_dev)
    block = start // 2
    blocks = n_dev * LON // 8
    copies = []
    for i in range(2):
        at = pl.multiple_of(lax.rem(block + i, blocks) * 8, 8)
        copies.append(
            pltpu.make_async_copy(
                ocean.at[pl.ds(at, 8), :], ocean_v.at[pl.ds(8 * i, 8), :], sems.at[i]
            )
        )
        copies[i].start()

    for side in range(2):

        @pl.when(hemi == side)
        def _(side=side):
            pltpu.make_async_copy((east, west)[side], first_v, sems.at[2]).start()
            pltpu.make_async_copy((west, east)[side], second_v, sems.at[3]).start()

    copies.append(pltpu.make_async_copy(east, first_v, sems.at[2]))
    copies.append(pltpu.make_async_copy(west, second_v, sems.at[3]))
    for copy in copies:
        copy.wait()
    offset = start * LON - block * 8
    for i in range(3 * LON):
        masks[i:i + 1, :] = ocean_v[pl.ds(offset + i, 1), :].astype(jnp.float32)

    def run(slot, side, own_ref, out_ref, cross_ref):
        def load(base):
            return [None] * LON + [own_ref[own_rows(base, n), :] for n in range(LON)]

        def store(base, level, cross, far):
            for n in range(LON):
                out_ref[own_rows(base, n), :] = level[n]
                if far is not None:
                    cross_ref[cross_rows(cross, n), :] = far[n]

        advance(slot, side, courant_ref, times_ref, masks, load, store)

    for side in range(2):

        @pl.when(hemi == side)
        def _(side=side):
            run(0, side, first_v, out0, cross0)
            run(1, side, second_v, out1, cross1)


def halo_load(halo_ref):
    def load(base):
        return [halo_ref[own_rows(base, n), :] for n in range(LON)] + [None] * LON

    return load


def stage_rows(slot, hemi, base, n):
    i = base // NF % 6
    forward = hemi if slot == 0 else 1 - hemi
    lon = LON - 1 - n if forward else n
    return pl.ds((base % NF) * QUARTER + i * LON + lon, 8, stride=QUARTER)


def quarter_copy(slot, toward, stage, out, sem):
    hemi = lax.axis_index("hemi")
    part = slot if toward else 1 - slot
    at = pl.multiple_of(2 * QUARTER * (hemi if toward else 1 - hemi) + QUARTER * part, 8)
    return pltpu.make_async_copy(
        stage.reshape(NF, QUARTER, LAT), out.at[:, pl.ds(at, QUARTER), :], sem
    )


def group_bases(slot, toward):
    first = 6 * toward if slot == 0 else 6 * (1 - toward)
    return [(i * NF + half * 8 + first * NF, i * NF + half * 8) for i in range(6) for half in range(2)]


def add_halo(slot, toward, side, rates, load, acc, stage, cross_in=None, cross_out=None):
    def store(base, level, cross, far):
        for n in range(LON):
            rows = stage_rows(slot, side, base, n)
            stage[rows, :] = acc[own_rows(base, n), :] + level[n]
            if far is not None:
                value = cross_in[cross_rows(cross, n), :]
                cross_out[cross_rows(cross, n), :] = total(value, far[n])

    advance(slot, side, *rates, load, store, (toward,))


def toward_kernel(courant_ref, times_ref, masks_ref, east, west, acc0, acc1, cross0, cross1, _,
                  ready0, ready1, cross_out):
    rates = (courant_ref, times_ref, masks_ref)
    for side in range(2):

        @pl.when(lax.axis_index("hemi") == side)
        def _(side=side):
            halo0, halo1 = (east, west) if side == 0 else (west, east)
            add_halo(0, 1, side, rates, halo_load(halo0), acc0, ready0, cross0, cross_out.at[0])
            add_halo(1, 1, side, rates, halo_load(halo1), acc1, ready1, cross1, cross_out.at[1])


def mark_kernel(*refs):
    refs[-1][...] = jnp.zeros((8, LAT), jnp.float32)


def away_kernel(courant_ref, times_ref, masks_ref, east, west, acc0, acc1, ready0, ready1,
                stage0, stage1, out, sems):
    copies = [quarter_copy(0, 1, ready0, out, sems.at[0]), quarter_copy(1, 1, ready1, out, sems.at[1])]
    for copy in copies:
        copy.start()
    rates = (courant_ref, times_ref, masks_ref)
    for side in range(2):

        @pl.when(lax.axis_index("hemi") == side)
        def _(side=side):
            halo0, halo1 = (east, west) if side == 0 else (west, east)
            add_halo(0, 0, side, rates, halo_load(halo0), acc0, stage0)
            add_halo(1, 0, side, rates, halo_load(halo1), acc1, stage1)

    for copy in copies:
        copy.wait()


def join_kernel(stage0, stage1, cross, _, out, ready0, ready1, sems):
    copies = []
    for slot, stage, ready in ((0, stage0, ready0), (1, stage1, ready1)):
        for side in range(2):

            @pl.when(lax.axis_index("hemi") == side)
            def _(side=side):
                first = 6 * slot * NF
                for i in range(6):
                    for half in range(2):
                        at = i * NF + half * 8
                        for n in range(LON):
                            rows = stage_rows(slot, side, first + at, n)
                            ready[rows, :] = stage[rows, :] + cross[1 - slot, cross_rows(at, n), :]

        copies.append(quarter_copy(slot, 0, ready, out, sems.at[slot]))
        copies[slot].start()
    for copy in copies:
        copy.wait()


SMEM = pl.BlockSpec(memory_space=pltpu.SMEM)
VMEM = pl.BlockSpec(memory_space=pltpu.VMEM)
HBM = pl.BlockSpec(memory_space=pltpu.HBM)


def params(mib=40):
    return pltpu.CompilerParams(vmem_limit_bytes=int(mib * MIB))


def cost(flops):
    return pl.CostEstimate(flops=int(flops), bytes_accessed=1000, transcendentals=0)


SOURCE_SCRATCH = [
    pltpu.VMEM((K * LON, LAT), jnp.float32),
    pltpu.VMEM((LON, LAT), jnp.float32),
    pltpu.VMEM((LON, LAT), jnp.int32),
    pltpu.VMEM((K,), jnp.float32),
    pltpu.VMEM((2 * K, K), jnp.int32),
    pltpu.VMEM((8, 2 * LAT), jnp.int32),
    pltpu.VMEM((LON, HALF, LAT), jnp.float32),
    pltpu.VMEM((LON, HALF, LAT), jnp.float32),
    pltpu.SemaphoreType.DMA((6 + 2 * LON,)),
    pltpu.VMEM((2 * K, 2 * K), jnp.bfloat16),
    pltpu.VMEM((K, 2 * K), jnp.bfloat16),
    pltpu.VMEM((K * LON, LAT), jnp.float32),
    pltpu.VMEM((SPLIT, 2 * K, PTS // SPLIT), jnp.bfloat16),
    pltpu.VMEM((SPLIT, 2 * K, PTS // SPLIT), jnp.float32),
    pltpu.VMEM((SPLIT, 2 * K, PTS // SPLIT), jnp.bfloat16),
    pltpu.VMEM((SPLIT, K, PTS // SPLIT), jnp.float32),
    pltpu.VMEM((K, LAT), jnp.float32),
]


def local(spectrum, wind_speed, src_counts, ocean_mask, growth, quadruplet, courant, freq_counts):
    n_dev = lax.axis_size("dev")
    half_shape = jax.ShapeDtypeStruct((LON * HALF, LAT), jnp.float32)
    cross_shape = jax.ShapeDtypeStruct((LON * GROUP, LAT), jnp.float32)
    mask_shape = jax.ShapeDtypeStruct((3 * LON, 2 * LAT), jnp.float32)
    out_shape = jax.ShapeDtypeStruct((NF, ND * LON, LAT), jnp.float32)
    given = (
        spectrum.reshape(K * LON, LAT), wind_speed, src_counts, growth,
        quadruplet.reshape(2 * K, K), ocean_mask,
    )

    east, west = pl.pallas_call(
        source_kernel,
        out_shape=(half_shape, half_shape),
        in_specs=[HBM] * 6,
        out_specs=(HBM, HBM),
        scratch_shapes=SOURCE_SCRATCH,
        compiler_params=params(56),
        cost_estimate=cost(6e9),
    )(*given)

    ring = range(n_dev)
    halo_east = lax.ppermute(east, "dev", [(i, (i + 1) % n_dev) for i in ring])
    halo_west = lax.ppermute(west, "dev", [(i, (i - 1) % n_dev) for i in ring])

    out0, out1, cross0, cross1, masks = pl.pallas_call(
        own_kernel,
        out_shape=(half_shape, half_shape, cross_shape, cross_shape, mask_shape),
        in_specs=[SMEM] * 2 + [HBM] * 3,
        out_specs=(VMEM,) * 5,
        scratch_shapes=[
            pltpu.VMEM((LON * HALF, LAT), jnp.float32),
            pltpu.VMEM((LON * HALF, LAT), jnp.float32),
            pltpu.VMEM((16, 2 * LAT), jnp.int32),
            pltpu.SemaphoreType.DMA((4,)),
        ],
        compiler_params=params(52.6),
        cost_estimate=cost(3e9),
    )(courant, freq_counts, ocean_mask, east, west)
    rates = (courant, freq_counts, masks)
    quarter_shape = jax.ShapeDtypeStruct((NF * QUARTER, LAT), jnp.float32)

    def tail(kernel, outs, count, *operands, **more):
        return pl.pallas_call(
            kernel,
            out_shape=outs,
            in_specs=[SMEM] * 2 + [VMEM] * (1 + count),
            compiler_params=params(),
            cost_estimate=cost(1e9),
            **more,
        )(*rates, *operands)

    def mark(*values):
        return pl.pallas_call(
            mark_kernel,
            out_shape=jax.ShapeDtypeStruct((8, LAT), jnp.float32),
            in_specs=[VMEM] * len(values),
            out_specs=VMEM,
            compiler_params=params(),
            cost_estimate=cost(1e8),
        )(*values)

    order = mark(halo_east, out0)
    both_shape = jax.ShapeDtypeStruct((2, LON * GROUP, LAT), jnp.float32)
    halos = (halo_east, halo_west, out0, out1)
    ready0, ready1, cross = tail(
        toward_kernel, (quarter_shape, quarter_shape, both_shape), 7, *halos, cross0, cross1, order,
        out_specs=(VMEM,) * 3,
    )
    cross = lax.ppermute(cross, "hemi", [(0, 1), (1, 0)])
    stage0, stage1, out = tail(
        away_kernel, (quarter_shape, quarter_shape, out_shape), 6, *halos, ready0, ready1,
        out_specs=(VMEM, VMEM, HBM), scratch_shapes=[pltpu.SemaphoreType.DMA((2,))],
    )
    out = pl.pallas_call(
        join_kernel,
        out_shape=out_shape,
        in_specs=[VMEM] * 3 + [HBM],
        out_specs=HBM,
        scratch_shapes=[
            pltpu.VMEM((NF * QUARTER, LAT), jnp.float32),
            pltpu.VMEM((NF * QUARTER, LAT), jnp.float32),
            pltpu.SemaphoreType.DMA((2,)),
        ],
        input_output_aliases={3: 0},
        compiler_params=params(),
    )(stage0, stage1, cross, out)
    return out.reshape(K, LON, LAT)


def solution(mesh):
    return jax.shard_map(
        local,
        mesh=mesh,
        in_specs=(
            P(None, "dev", "hemi"),
            P("dev", "hemi"),
            P("dev", "hemi"),
            P(),
            P(),
            P(),
            P(),
            P(),
        ),
        out_specs=P(None, "dev", "hemi"),
        check_vma=False,
    )
```

```python
import functools
import math

import jax
import jax.numpy as jnp
from jax import lax
from jax.experimental import pallas as pl
from jax.experimental.pallas import tpu as pltpu
from jax.sharding import PartitionSpec as P

ND = 24
NF = 16
K = ND * NF
LON = 4
LAT = 128
PTS = LON * LAT
SRC_MAX = 3
SPLIT = 2
GATHER_BLOCK = 128
SCATTER_BLOCK = 128
SUB_MAX = 4
HALF = K // 2
GROUP = 6 * NF
QUARTER = 6 * LON
coupling = 0.25
breaking = 0.5
spread = 0.7
MIB = 1024 * 1024


def direction(j, hemi):
    return lax.rem(18 + j + 12 * hemi, ND)


def split(value):
    high = value.astype(jnp.bfloat16)
    low = (value - high.astype(jnp.float32)).astype(jnp.bfloat16)
    return high, low


def source_terms(
    hemi, dev, ocean_ref, growth_ref, wind_ref, count_ref, quad_ref, spec_ref, waits, send,
    gather_m, scatter_m, energy, parts, paired, terms, moved, grow,
):
    nt = (((1,), (1,)), ((), ()))
    eye = (
        lax.broadcasted_iota(jnp.int32, (K, K), 0) == lax.broadcasted_iota(jnp.int32, (K, K), 1)
    ).astype(jnp.float32)
    eye_bf = eye.astype(jnp.bfloat16)
    waits["small"]()
    rest = jnp.broadcast_to(growth_ref[...].reshape(1, K), (LAT, K))
    column = None
    for _ in range(3):
        part = rest.astype(jnp.bfloat16)
        rest = rest - part.astype(jnp.float32)
        term = lax.dot_general(eye_bf, part, nt, preferred_element_type=jnp.float32)
        column = term if column is None else column + term
    grow[...] = column

    winds = []
    oceans = []
    counts = []
    for lon in range(LON):
        winds.append(wind_ref[lon:lon + 1, :])
        counts.append(count_ref[lon:lon + 1, :])
        row = ocean_ref[pl.ds(LON * lax.rem(dev, 2) + lon, 1), :].astype(jnp.float32)
        oceans.append(jnp.where(hemi == 0, row[:, :LAT], row[:, LAT:]))
    steps = [oceans[lon] / counts[lon].astype(jnp.float32) for lon in range(LON)]

    waits["quad"]()
    sides = []
    for side in range(2):
        rows = quad_ref[side * K:(side + 1) * K, :].astype(jnp.float32).astype(jnp.bfloat16)
        gather_m[side * K:(side + 1) * K, :K] = rows
        gather_m[side * K:(side + 1) * K, K:] = rows
        sides.append(rows)
    back = lax.dot_general(eye_bf, sides[0] + sides[1], nt, preferred_element_type=jnp.float32)
    back = (coupling * (back - 2.0 * eye)).astype(jnp.bfloat16)
    scatter_m[:, :K] = back
    scatter_m[:, K:] = back

    waits["spec"]()
    per = LON // SPLIT
    for part in range(SPLIT):
        for i in range(K // NF):
            for sub in range(per):
                lon = part * per + sub
                cols = slice(sub * LAT, (sub + 1) * LAT)
                value = spec_ref[pl.ds(i * NF * LON + lon, NF, stride=LON), :] * oceans[lon]
                energy[lon * K + i * NF:lon * K + (i + 1) * NF, :] = value
                high, low = split(value)
                parts[part, i * NF:(i + 1) * NF, cols] = high
                parts[part, K + i * NF:K + (i + 1) * NF, cols] = low

    def gather_rows(part, rows):
        def run():
            paired[part, rows, :] = jnp.dot(
                gather_m[rows, :], parts[part], preferred_element_type=jnp.float32
            )
        return run

    def scatter_rows(part, rows):
        def run():
            moved[part, rows, :] = jnp.dot(
                scatter_m[rows, :], terms[part], preferred_element_type=jnp.float32
            )
        return run

    def quad_rows(part, i):
        def run():
            at = slice(i * NF, (i + 1) * NF)
            below = slice(K + i * NF, K + (i + 1) * NF)
            for sub in range(per):
                lon = part * per + sub
                cols = slice(sub * LAT, (sub + 1) * LAT)
                value = energy[lon * K + i * NF:lon * K + (i + 1) * NF, :]
                plus = paired[part, at, cols]
                minus = paired[part, below, cols]
                term = value * (value * (plus + minus) - 2.0 * (plus * minus))
                high, low = split(term)
                terms[part, at, cols] = high
                terms[part, below, cols] = low
        return run

    def update_rows(part, i, cycle):
        def run():
            at = slice(i * NF, (i + 1) * NF)
            below = slice(K + i * NF, K + (i + 1) * NF)
            rate = grow[at, :]
            for sub in range(per):
                lon = part * per + sub
                cols = slice(sub * LAT, (sub + 1) * LAT)
                value = energy[lon * K + i * NF:lon * K + (i + 1) * NF, :]
                tendency = value * (rate * winds[lon] - breaking * value)
                tendency = tendency + moved[part, at, cols]
                value = jnp.where(cycle < counts[lon], value + steps[lon] * tendency, value)
                energy[lon * K + i * NF:lon * K + (i + 1) * NF, :] = value
                if cycle < SRC_MAX - 1:
                    high, low = split(value)
                    parts[part, at, cols] = high
                    parts[part, below, cols] = low
        return run

    def weave(dots, rows):
        per_dot = -(-len(rows) // max(len(dots), 1))
        for n in range(max(len(dots), 1)):
            for dot in dots[n:n + 1]:
                dot()
            for row in rows[n * per_dot:(n + 1) * per_dot]:
                row()

    def blocks(make, part, count, size):
        return [make(part, slice(n, n + size)) for n in range(0, count, size)]

    steps_of = K // NF
    weave(blocks(gather_rows, 0, 2 * K, GATHER_BLOCK), [])
    for cycle in range(SRC_MAX):
        weave(blocks(gather_rows, 1, 2 * K, GATHER_BLOCK), [quad_rows(0, i) for i in range(steps_of)])
        weave(blocks(scatter_rows, 0, K, SCATTER_BLOCK), [quad_rows(1, i) for i in range(steps_of)])
        weave(blocks(scatter_rows, 1, K, SCATTER_BLOCK), [update_rows(0, i, cycle) for i in range(steps_of)])
        if cycle < SRC_MAX - 1:
            weave(blocks(gather_rows, 0, 2 * K, GATHER_BLOCK), [update_rows(1, i, cycle) for i in range(steps_of)])
        else:
            for lon in range(per):
                send(lon)
            weave([], [update_rows(1, i, cycle) for i in range(steps_of)])
            for lon in range(per, LON):
                send(lon)


def source_kernel(
    spec, wind, count, growth, quad, ocean, east, west,
    spec_v, wind_v, count_v, growth_v, quad_v, ocean_v, first_v, second_v, sems, *work,
):
    hemi = lax.axis_index("hemi")
    dev = lax.axis_index("dev")
    block = pl.multiple_of(dev // 2 * 8, 8)
    small = [
        pltpu.make_async_copy(growth, growth_v, sems.at[2]),
        pltpu.make_async_copy(wind, wind_v, sems.at[3]),
        pltpu.make_async_copy(count, count_v, sems.at[4]),
        pltpu.make_async_copy(ocean.at[pl.ds(block, 8), :], ocean_v, sems.at[5]),
    ]
    large = {
        "quad": pltpu.make_async_copy(quad, quad_v, sems.at[0]),
        "spec": pltpu.make_async_copy(spec, spec_v, sems.at[1]),
    }
    large["quad"].start()
    for copy in small:
        copy.start()
    large["spec"].start()

    def wait_small():
        for copy in small:
            copy.wait()

    waits = {"small": wait_small, "quad": large["quad"].wait, "spec": large["spec"].wait}
    outs = []

    def send(lon):
        for slot, source in enumerate((first_v, second_v)):
            forward = hemi if slot == 0 else 1 - hemi
            n = lon + forward * (LON - 1 - 2 * lon)
            rows = pl.ds(pl.multiple_of(n * HALF, HALF), HALF)
            for jj in range(12):
                d = direction(jj + 12 * slot, hemi)
                source[lon, jj * NF:(jj + 1) * NF, :] = work[2][pl.ds(lon * K + d, NF, stride=ND), :]
            for side in range(2):
                copy = pltpu.make_async_copy(
                    source.at[lon], (east, west)[slot ^ side].at[rows, :], sems.at[6 + 2 * lon + slot]
                )
                pl.when(hemi == side)(copy.start)
            outs.append(copy)

    source_terms(
        hemi, dev, ocean_v, growth_v, wind_v, count_v, quad_v, spec_v, waits, send, *work,
    )
    for copy in outs:
        copy.wait()


BATCH = (12, 4)


def fine(value, active):
    return value if active is None else jnp.where(active, value, 0.0)


def total(*terms):
    terms = [term for term in terms if term is not None]
    if not terms:
        return None
    out = terms[0]
    for term in terms[1:]:
        out = out + term
    return out


def times(rate, value):
    return None if value is None else rate * value


def advance(slot, hemi, courant_ref, times_ref, masks_ref, load, store, which=(1, 0)):
    forward = hemi if slot == 0 else 1 - hemi
    lanes = slice(hemi * LAT, (hemi + 1) * LAT)
    far_lanes = slice((1 - hemi) * LAT, (2 - hemi) * LAT)
    masks = []
    far_masks = []
    for n in range(-LON, LON):
        at = LON + (n if forward == 0 else LON - 1 - n)
        masks.append(jnp.broadcast_to(masks_ref[at:at + 1, lanes], (8, LAT)))
        far_masks.append(jnp.broadcast_to(masks_ref[at:at + 1, far_lanes], (8, LAT)))
    lane = lax.broadcasted_iota(jnp.int32, (8, LAT), 1)
    row8 = lax.broadcasted_iota(jnp.int32, (8, LAT), 0)
    rates = []
    for half in range(2):
        courant = jnp.zeros((8, LAT), jnp.float32)
        count = jnp.zeros((8, LAT), jnp.int32)
        for r in range(8):
            courant = jnp.where(row8 == r, courant_ref[half * 8 + r], courant)
            count = jnp.where(row8 == r, times_ref[half * 8 + r], count)
        rates.append((spread * courant, [None] + [count > t for t in range(1, SUB_MAX)]))
    for toward in which:
        up = hemi if toward == 0 else 1 - hemi
        shift = 1 if up else LAT - 1
        edge = lane == (0 if up else LAT - 1)
        batch = BATCH[toward]
        both = [(half, i) for half in range(2) for i in range(6)]
        for first in range(0, 12, batch):
            groups = []
            for half, i in both[first:first + batch]:
                speed, active = rates[half]
                jj = i + (6 * toward if slot == 0 else 6 * (1 - toward))
                angle = 2.0 * math.pi * ((18 + jj + 12 * slot) % ND + 0.5) / ND
                cx = speed * abs(math.cos(angle))
                cy = speed * abs(math.sin(angle))
                base = jj * NF + half * 8
                cross = i * NF + half * 8
                groups.append((base, cross, cx, cy, 1.0 - cx - cy, load(base), [None] * (2 * LON), active))
            for t in range(SUB_MAX):
                for n in range(2 * LON - 1, t, -1):
                    for base, cross, cx, cy, stay, level, far, active in groups:
                        rolled = None if level[n] is None else pltpu.roll(level[n], shift, 1)
                        south = None if rolled is None else jnp.where(edge, 0.0, rolled)
                        value = total(times(stay, level[n]), times(cx, level[n - 1]), times(cy, south))
                        if toward:
                            inflow = None
                            if far[n] is not None:
                                inflow = jnp.where(edge, rolled, pltpu.roll(far[n], shift, 1))
                            elif rolled is not None:
                                inflow = jnp.where(edge, rolled, 0.0)
                            other = total(times(stay, far[n]), times(cx, far[n - 1]), times(cy, inflow))
                            if other is not None:
                                other = far_masks[n] * other
                                if t:
                                    old = 0.0 if far[n] is None else far[n]
                                    other = jnp.where(active[t], other, old)
                                far[n] = other
                        if value is not None:
                            value = masks[n] * value
                            if t:
                                old = 0.0 if level[n] is None else level[n]
                                value = jnp.where(active[t], value, old)
                            level[n] = value
            for base, cross, cx, cy, stay, level, far, active in groups:
                store(base, level[LON:], cross, far[LON:] if toward else None)


def own_rows(base, n):
    return slice(n * HALF + base, n * HALF + base + 8)


def cross_rows(cross, n):
    return slice(n * GROUP + cross, n * GROUP + cross + 8)


def own_kernel(
    courant_ref, times_ref, ocean, east, west, out0, out1, cross0, cross1, masks,
    first_v, second_v, ocean_v, sems,
):
    hemi = lax.axis_index("hemi")
    dev = lax.axis_index("dev")
    n_dev = lax.axis_size("dev")
    start = lax.rem(dev + n_dev - 1, n_dev)
    block = start // 2
    blocks = n_dev * LON // 8
    copies = []
    for i in range(2):
        at = pl.multiple_of(lax.rem(block + i, blocks) * 8, 8)
        copies.append(
            pltpu.make_async_copy(
                ocean.at[pl.ds(at, 8), :], ocean_v.at[pl.ds(8 * i, 8), :], sems.at[i]
            )
        )
        copies[i].start()

    for side in range(2):

        @pl.when(hemi == side)
        def _(side=side):
            pltpu.make_async_copy((east, west)[side], first_v, sems.at[2]).start()
            pltpu.make_async_copy((west, east)[side], second_v, sems.at[3]).start()

    copies.append(pltpu.make_async_copy(east, first_v, sems.at[2]))
    copies.append(pltpu.make_async_copy(west, second_v, sems.at[3]))
    for copy in copies:
        copy.wait()
    offset = start * LON - block * 8
    for i in range(3 * LON):
        masks[i:i + 1, :] = ocean_v[pl.ds(offset + i, 1), :].astype(jnp.float32)

    def run(slot, side, own_ref, out_ref, cross_ref):
        def load(base):
            return [None] * LON + [own_ref[own_rows(base, n), :] for n in range(LON)]

        def store(base, level, cross, far):
            for n in range(LON):
                out_ref[own_rows(base, n), :] = level[n]
                if far is not None:
                    cross_ref[cross_rows(cross, n), :] = far[n]

        advance(slot, side, courant_ref, times_ref, masks, load, store)

    for side in range(2):

        @pl.when(hemi == side)
        def _(side=side):
            run(0, side, first_v, out0, cross0)
            run(1, side, second_v, out1, cross1)


def halo_load(halo_ref):
    def load(base):
        return [halo_ref[own_rows(base, n), :] for n in range(LON)] + [None] * LON

    return load


def stage_rows(slot, hemi, base, n):
    i = base // NF % 6
    forward = hemi if slot == 0 else 1 - hemi
    lon = LON - 1 - n if forward else n
    return pl.ds((base % NF) * QUARTER + i * LON + lon, 8, stride=QUARTER)


def quarter_copy(slot, toward, stage, out, sem):
    hemi = lax.axis_index("hemi")
    part = slot if toward else 1 - slot
    at = pl.multiple_of(2 * QUARTER * (hemi if toward else 1 - hemi) + QUARTER * part, 8)
    return pltpu.make_async_copy(
        stage.reshape(NF, QUARTER, LAT), out.at[:, pl.ds(at, QUARTER), :], sem
    )


def group_bases(slot, toward):
    first = 6 * toward if slot == 0 else 6 * (1 - toward)
    return [(i * NF + half * 8 + first * NF, i * NF + half * 8) for i in range(6) for half in range(2)]


def add_halo(slot, toward, side, rates, load, acc, stage, cross_in=None, cross_out=None):
    def store(base, level, cross, far):
        for n in range(LON):
            rows = stage_rows(slot, side, base, n)
            stage[rows, :] = acc[own_rows(base, n), :] + level[n]
            if far is not None:
                value = cross_in[cross_rows(cross, n), :]
                cross_out[cross_rows(cross, n), :] = total(value, far[n])

    advance(slot, side, *rates, load, store, (toward,))


def toward_kernel(courant_ref, times_ref, masks_ref, east, west, acc0, acc1, cross0, cross1, _,
                  ready0, ready1, cross_out):
    rates = (courant_ref, times_ref, masks_ref)
    for side in range(2):

        @pl.when(lax.axis_index("hemi") == side)
        def _(side=side):
            halo0, halo1 = (east, west) if side == 0 else (west, east)
            add_halo(0, 1, side, rates, halo_load(halo0), acc0, ready0, cross0, cross_out.at[0])
            add_halo(1, 1, side, rates, halo_load(halo1), acc1, ready1, cross1, cross_out.at[1])


def mark_kernel(*refs):
    refs[-1][...] = jnp.zeros((8, LAT), jnp.float32)


def away_kernel(courant_ref, times_ref, masks_ref, east, west, acc0, acc1, ready0, ready1,
                stage0, stage1, out, sems):
    copies = [quarter_copy(0, 1, ready0, out, sems.at[0]), quarter_copy(1, 1, ready1, out, sems.at[1])]
    for copy in copies:
        copy.start()
    rates = (courant_ref, times_ref, masks_ref)
    for side in range(2):

        @pl.when(lax.axis_index("hemi") == side)
        def _(side=side):
            halo0, halo1 = (east, west) if side == 0 else (west, east)
            add_halo(0, 0, side, rates, halo_load(halo0), acc0, stage0)
            add_halo(1, 0, side, rates, halo_load(halo1), acc1, stage1)

    for copy in copies:
        copy.wait()


def join_kernel(stage0, stage1, cross, _, out, ready0, ready1, sems):
    copies = []
    for slot, stage, ready in ((0, stage0, ready0), (1, stage1, ready1)):
        for side in range(2):

            @pl.when(lax.axis_index("hemi") == side)
            def _(side=side):
                first = 6 * slot * NF
                for i in range(6):
                    for half in range(2):
                        at = i * NF + half * 8
                        for n in range(LON):
                            rows = stage_rows(slot, side, first + at, n)
                            ready[rows, :] = stage[rows, :] + cross[1 - slot, cross_rows(at, n), :]

        copies.append(quarter_copy(slot, 0, ready, out, sems.at[slot]))
        copies[slot].start()
    for copy in copies:
        copy.wait()


SMEM = pl.BlockSpec(memory_space=pltpu.SMEM)
VMEM = pl.BlockSpec(memory_space=pltpu.VMEM)
HBM = pl.BlockSpec(memory_space=pltpu.HBM)


def params(mib=40):
    return pltpu.CompilerParams(vmem_limit_bytes=int(mib * MIB))


def cost(flops):
    return pl.CostEstimate(flops=int(flops), bytes_accessed=1000, transcendentals=0)


SOURCE_SCRATCH = [
    pltpu.VMEM((K * LON, LAT), jnp.float32),
    pltpu.VMEM((LON, LAT), jnp.float32),
    pltpu.VMEM((LON, LAT), jnp.int32),
    pltpu.VMEM((K,), jnp.float32),
    pltpu.VMEM((2 * K, K), jnp.int32),
    pltpu.VMEM((8, 2 * LAT), jnp.int32),
    pltpu.VMEM((LON, HALF, LAT), jnp.float32),
    pltpu.VMEM((LON, HALF, LAT), jnp.float32),
    pltpu.SemaphoreType.DMA((6 + 2 * LON,)),
    pltpu.VMEM((2 * K, 2 * K), jnp.bfloat16),
    pltpu.VMEM((K, 2 * K), jnp.bfloat16),
    pltpu.VMEM((K * LON, LAT), jnp.float32),
    pltpu.VMEM((SPLIT, 2 * K, PTS // SPLIT), jnp.bfloat16),
    pltpu.VMEM((SPLIT, 2 * K, PTS // SPLIT), jnp.float32),
    pltpu.VMEM((SPLIT, 2 * K, PTS // SPLIT), jnp.bfloat16),
    pltpu.VMEM((SPLIT, K, PTS // SPLIT), jnp.float32),
    pltpu.VMEM((K, LAT), jnp.float32),
]


def local(spectrum, wind_speed, src_counts, ocean_mask, growth, quadruplet, courant, freq_counts):
    n_dev = lax.axis_size("dev")
    half_shape = jax.ShapeDtypeStruct((LON * HALF, LAT), jnp.float32)
    cross_shape = jax.ShapeDtypeStruct((LON * GROUP, LAT), jnp.float32)
    mask_shape = jax.ShapeDtypeStruct((3 * LON, 2 * LAT), jnp.float32)
    out_shape = jax.ShapeDtypeStruct((NF, ND * LON, LAT), jnp.float32)
    given = (
        spectrum.reshape(K * LON, LAT), wind_speed, src_counts, growth,
        quadruplet.reshape(2 * K, K), ocean_mask,
    )

    east, west = pl.pallas_call(
        source_kernel,
        out_shape=(half_shape, half_shape),
        in_specs=[HBM] * 6,
        out_specs=(HBM, HBM),
        scratch_shapes=SOURCE_SCRATCH,
        compiler_params=params(56),
        cost_estimate=cost(6e9),
    )(*given)

    ring = range(n_dev)
    halo_east = lax.ppermute(east, "dev", [(i, (i + 1) % n_dev) for i in ring])
    halo_west = lax.ppermute(west, "dev", [(i, (i - 1) % n_dev) for i in ring])

    out0, out1, cross0, cross1, masks = pl.pallas_call(
        own_kernel,
        out_shape=(half_shape, half_shape, cross_shape, cross_shape, mask_shape),
        in_specs=[SMEM] * 2 + [HBM] * 3,
        out_specs=(VMEM,) * 5,
        scratch_shapes=[
            pltpu.VMEM((LON * HALF, LAT), jnp.float32),
            pltpu.VMEM((LON * HALF, LAT), jnp.float32),
            pltpu.VMEM((16, 2 * LAT), jnp.int32),
            pltpu.SemaphoreType.DMA((4,)),
        ],
        compiler_params=params(52.6),
        cost_estimate=cost(3e9),
    )(courant, freq_counts, ocean_mask, east, west)
    rates = (courant, freq_counts, masks)
    quarter_shape = jax.ShapeDtypeStruct((NF * QUARTER, LAT), jnp.float32)

    def tail(kernel, outs, count, *operands, **more):
        return pl.pallas_call(
            kernel,
            out_shape=outs,
            in_specs=[SMEM] * 2 + [VMEM] * (1 + count),
            compiler_params=params(),
            cost_estimate=cost(1e9),
            **more,
        )(*rates, *operands)

    def mark(*values):
        return pl.pallas_call(
            mark_kernel,
            out_shape=jax.ShapeDtypeStruct((8, LAT), jnp.float32),
            in_specs=[VMEM] * len(values),
            out_specs=VMEM,
            compiler_params=params(),
            cost_estimate=cost(1e8),
        )(*values)

    order = mark(halo_east, out0)
    both_shape = jax.ShapeDtypeStruct((2, LON * GROUP, LAT), jnp.float32)
    halos = (halo_east, halo_west, out0, out1)
    ready0, ready1, cross = tail(
        toward_kernel, (quarter_shape, quarter_shape, both_shape), 7, *halos, cross0, cross1, order,
        out_specs=(VMEM,) * 3,
    )
    cross = lax.ppermute(cross, "hemi", [(0, 1), (1, 0)])
    stage0, stage1, out = tail(
        away_kernel, (quarter_shape, quarter_shape, out_shape), 6, *halos, ready0, ready1,
        out_specs=(VMEM, VMEM, HBM), scratch_shapes=[pltpu.SemaphoreType.DMA((2,))],
    )
    out = pl.pallas_call(
        join_kernel,
        out_shape=out_shape,
        in_specs=[VMEM] * 3 + [HBM],
        out_specs=HBM,
        scratch_shapes=[
            pltpu.VMEM((NF * QUARTER, LAT), jnp.float32),
            pltpu.VMEM((NF * QUARTER, LAT), jnp.float32),
            pltpu.SemaphoreType.DMA((2,)),
        ],
        input_output_aliases={3: 0},
        compiler_params=params(),
    )(stage0, stage1, cross, out)
    return out.reshape(K, LON, LAT)


def solution(mesh):
    return jax.shard_map(
        local,
        mesh=mesh,
        in_specs=(
            P(None, "dev", "hemi"),
            P("dev", "hemi"),
            P("dev", "hemi"),
            P(),
            P(),
            P(),
            P(),
            P(),
        ),
        out_specs=P(None, "dev", "hemi"),
        check_vma=False,
    )
```
